32 devices in a mesh: fsdp: 16 (over z, y, core), rep: 2 (over x).
Axes of the slice: x: 2, y: 2, z: 4, core: 2. Of those that a mesh axis runs over, the one named last changes fastest.
Arguments:
- patches: bfloat16 [8192, 2048], P(('fsdp', 'rep')), may hold values from -6 to 6
- cotangent: bfloat16 [8192, 2048], P(('fsdp', 'rep')), may hold values from -0.0625 to 0.0625
- student: float32 [2048, 2048], P('fsdp'), may hold values from -6 to 6
- first_moment: float32 [2048, 2048], P('fsdp'), may hold values from -4 to 4
- second_moment: float32 [2048, 2048], P('fsdp'), may hold values from 0.0005 to 0.03
- teacher: float32 [2048, 2048], P('fsdp'), may hold values from -6 to 6
Outputs:
- features: bfloat16 [8192, 2048], P(('fsdp', 'rep'))
- new_student: float32 [2048, 2048], P('fsdp')
- new_first: float32 [2048, 2048], P('fsdp')
- new_second: float32 [2048, 2048], P('fsdp')
- new_teacher: float32 [2048, 2048], P('fsdp')
The draws below stay inside these ranges and needn't reach their ends.
All inputs are finite; a program needn't handle non-finite values.
Results may differ from the reference program's by a relative error of at most 0.006.
Values may be sent and summed in bfloat16 or wider, within the bound.
No kernel may reach another device: no remote copies, remote signals or barrier semaphores. Data moves between devices by JAX's collectives and lax.ppermute only.
A program may use at most 128 MiB of HBM per device.

```python
import math
import jax
import jax.numpy as jnp
from jax import lax

FEAT = 2048
OUTW = 2048
TOK_DEV = 256
STEP = 100
TOKENS = 8192
N_FSDP = 16
N_REP = 2


def with_spikes(result, key, source, target, parts, factor):
    def block_of(axis_at):
        return (jnp.arange(result.shape[axis_at]) // (result.shape[axis_at] // parts)).reshape((-1,) + (1,) * (result.ndim - 1 - axis_at))

    one_side = jax.random.permutation(key, parts)[block_of(target)]
    second = (block_of(target) + parts // 2) % parts
    return jnp.where((block_of(source) == one_side) | (block_of(source) == second), factor * result, result)


def steps_of(key, dims, cuts, smallest, largest):
    def one(dim, parts):
        steps = jax.random.uniform(jax.random.fold_in(jax.random.fold_in(key, 6), dim), (parts,), jnp.float32, smallest / len(cuts), largest / len(cuts))
        return jnp.repeat(jnp.exp(steps), dims[dim] // parts).reshape((-1,) + (1,) * (len(dims) - dim - 1))

    gain = one(*cuts[0])
    for cut in cuts[1:]:
        gain = gain * one(*cut)
    return gain


def scatter_about(own_key, extent, scale, bound, pieces=(), kind=jnp.bfloat16):
    values = scale * jax.random.normal(own_key, extent, jnp.float32)
    if pieces:
        values = values * steps_of(own_key, extent, pieces, -0.22, 0.18)
    return jnp.clip(values, -bound, bound).astype(kind)


def noise_with(own_key, shape, width, limit, shards, heavy, dtype=jnp.bfloat16):
    array = width * jax.random.normal(own_key, shape, jnp.float32)
    if shards:
        array = array * steps_of(own_key, shape, shards, -0.22, 0.18)
    return jnp.clip(with_spikes(array, jax.random.fold_in(own_key, 3), *heavy), -limit, limit).astype(dtype)


def setup_inputs(seed: int = 0) -> dict:
    streams_of = jax.random.split(jax.random.key(seed), 7)
    patches = noise_with(streams_of[0], (TOKENS, FEAT), 1.0, 6.0, ((0, 32),), (0, 1, 32, 2.75))
    cotangent = scatter_about(streams_of[1], (TOKENS, OUTW), TOKENS ** -0.5, 0.0625, ((0, 32),))
    student = scatter_about(streams_of[2], (FEAT, OUTW), 1.0, 6.0, ((0, 16),), jnp.float32)
    first_moment = scatter_about(streams_of[3], (FEAT, OUTW), 0.3, 4.0, ((0, 16),), jnp.float32)
    second_moment = jnp.clip(jnp.exp(math.log(0.03) - 4.0943445 * jax.random.uniform(streams_of[4], (FEAT, OUTW), jnp.float32) ** steps_of(streams_of[4], (FEAT, OUTW), ((0, 16),), -0.2, 0.2)), 0.0005, 0.03)
    teacher = scatter_about(streams_of[5], (FEAT, OUTW), 1.0, 6.0, ((0, 16),), jnp.float32)
    return {"patches": patches, "cotangent": cotangent, "student": student, "first_moment": first_moment, "second_moment": second_moment, "teacher": teacher}


beta_one = 0.9
beta_two = 0.999
adam_eps = 1e-08
learn_rate = 0.1
decay_rate = 0.04
ema_keep = 0.994

def reference(patches, cotangent, student, first_moment, second_moment, teacher):
    teacher_weights = teacher.astype(jnp.bfloat16)
    features = (jnp.dot(patches, teacher_weights, preferred_element_type=jnp.float32) * FEAT ** (-0.5)).astype(jnp.bfloat16)
    device_count = N_FSDP * N_REP
    split_patches = patches.reshape(device_count, TOK_DEV, FEAT)
    split_cotangent = cotangent.reshape(device_count, TOK_DEV, OUTW)

    def add_term(total, pair):
        term = jnp.dot(pair[0].T, pair[1], preferred_element_type=jnp.float32).astype(jnp.bfloat16)
        return (total + term.astype(jnp.float32), None)
    gradient, unused = lax.scan(add_term, jnp.zeros((FEAT, OUTW), jnp.float32), (split_patches, split_cotangent))
    new_first = beta_one * first_moment + (1.0 - beta_one) * gradient
    new_second = beta_two * second_moment + (1.0 - beta_two) * gradient * gradient
    corr_one = 1.0 - beta_one ** STEP
    corr_two = 1.0 - beta_two ** STEP
    direction = new_first / corr_one / (jnp.sqrt(new_second / corr_two) + adam_eps)
    new_student = student - learn_rate * (direction + decay_rate * student)
    new_teacher = ema_keep * teacher + (1.0 - ema_keep) * new_student
    return (features, new_student, new_first, new_second, new_teacher)
```

```python
import math

import jax
import jax.numpy as jnp
from jax import lax
from jax.experimental import pallas as pl
from jax.experimental.pallas import tpu as pltpu
from jax.sharding import PartitionSpec as P

STEP = 100

beta_one = 0.9
beta_two = 0.999
adam_eps = 1e-08
learn_rate = 0.1
decay_rate = 0.04
ema_keep = 0.994

bf16, f32 = jnp.bfloat16, jnp.float32
VMEM = pl.BlockSpec(memory_space=pltpu.VMEM)


def call(name, body, outs, inputs, scratch=()):
    shapes = [jax.ShapeDtypeStruct(*out) for out in outs]
    moved = sum(a.size * a.dtype.itemsize for a in (*inputs, *shapes))
    held = sum(4 * math.prod(getattr(s, "shape", ())) for s in scratch)
    with jax.named_scope(name):
        return pl.pallas_call(
            body,
            out_shape=shapes,
            in_specs=[VMEM] * len(inputs),
            out_specs=[VMEM] * len(shapes),
            scratch_shapes=list(scratch),
            cost_estimate=pl.CostEstimate(flops=1, bytes_accessed=1, transcendentals=0),
            compiler_params=pltpu.CompilerParams(vmem_limit_bytes=moved + held + 4 * 2**20),
        )(*inputs)


def after(value, *others):
    return lax.optimization_barrier((value, *others))[0]


def aligned(index, size):
    return pl.ds(pl.multiple_of(index * size, size), size)


def solution(mesh):
    n, r = mesh.shape["fsdp"], mesh.shape["rep"]
    nz = 4
    ny = n // (2 * nz)
    pair_groups = r // 2

    def send(value, move):
        perm = []
        for f in range(n):
            for p in range(r):
                z, y, c = f // (2 * ny), f // 2 % ny, f % 2
                z, y, c, g, h = move(z, y, c, p // 2, p % 2)
                perm.append((f * r + p, ((z * ny + y) * 2 + c) * r + g * 2 + h))
        return lax.ppermute(value, ("fsdp", "rep"), perm)

    def sibling(z, y, c, g, h):
        return z, y, 1 - c, g, h

    def partner(z, y, c, g, h):
        return z, y, c, g, 1 - h

    def diagonal(z, y, c, g, h):
        return z, y, 1 - c, g, 1 - h

    def along_z(d):
        return lambda z, y, c, g, h: ((z + d) % nz, y, c, g, h)

    def across_z(d):
        return lambda z, y, c, g, h: (z ^ d, y, c, g, h)

    def along_y(d):
        return lambda z, y, c, g, h: (z, (y + d) % ny, c, g, h)

    def along_g(d):
        return lambda z, y, c, g, h: (z, y, c, (g + d) % pair_groups, h)

    def place():
        f = lax.axis_index("fsdp")
        core = lax.rem(f, 2)
        return f // (2 * ny), lax.rem(f // 2, ny), core, lax.rem(lax.axis_index("rep"), 2) * 2 + core

    def per_device(patches, cotangent, student, first_moment, second_moment, teacher):
        tokens, feat = patches.shape
        outw = cotangent.shape[1]
        rows = teacher.shape[0]
        part = outw // 4
        span = feat // nz
        g_order = [3, 2, 1, 0]
        lead = 2 * part

        def cut_body(p, c, first, near, c_own, *rest):
            z, y, core, q = place()
            first[:, :lead] = c[:, aligned(1 - q // 2, lead)]
            for k, dz in enumerate(g_order):
                block = p[:, aligned(z ^ dz, span)]
                near[:, k * span : (k + 1) * span] = block
                if k == 0:
                    first[:, lead:] = block
                else:
                    rest[k - 1][...] = block
            near[:, feat:] = c[:, aligned(q ^ 1, part)]
            c_own[...] = c[:, aligned(q, part)]

        def split_body(message, c_sib, c_here, block):
            z, y, core, q = place()
            c_sib[...] = message[:, aligned(1 - core, part)]
            c_here[...] = message[:, aligned(core, part)]
            block[...] = message[:, lead:]

        clock = []

        def run(name, body, outs, inputs, *scratch, **options):
            first = after(inputs[0], *clock) if clock else inputs[0]
            out = call(name, body, outs, [first, *inputs[1:]], *scratch, **options)
            clock[:] = out[:1]
            return out

        def start(value, move, *others):
            return send(after(value, *others) if others else value, move)

        def wait(*values):
            clock.extend(values)

        def cast_body(t, same, other):
            z, y, core, q = place()
            same[...] = t[:, aligned(q, part)].astype(bf16)
            other[...] = t[:, aligned(q ^ 1, part)].astype(bf16)

        def join_body(same, sib, out):
            z, y, core, q = place()
            out[aligned(core, rows), :] = same[...]
            out[aligned(1 - core, rows), :] = sib[...]

        def stack_body(*refs):
            for k, ref in enumerate(refs[:-1]):
                refs[-1][k * 2 * rows : (k + 1) * 2 * rows, :] = ref[...]

        def terms_body(k):
            def body(own, sib, par, dia, c0, c_par, c_dia, *outs):
                z, y, core, q = place()
                whole = outs[-1]
                near = slice(k * span, (k + 1) * span)
                total = None
                for p, c in (
                    (own[:, near], c0[...]),
                    (sib[:, near], sib[:, feat:]),
                    (par[...], c_par[...]),
                    (dia[...], c_dia[...]),
                ):
                    term = lax.dot_general(
                        p, c, (((0,), (0,)), ((), ())), preferred_element_type=f32
                    )
                    total = term if total is None else total + term
                whole[...] = total
                for dy in range(ny):
                    block = whole[aligned(lax.rem(y + dy, ny), 2 * rows), :]
                    outs[dy][...] = block.astype(outs[dy].dtype)

            return body

        def gradient_block(k):
            dz = g_order[k]
            terms[dz] = run(
                "gradient_block",
                terms_body(k),
                [((2 * rows, part), f32)] + [((2 * rows, part), bf16)] * (ny - 1),
                [near_own, near_sib, far_par[k], far_dia[k], c_own, c_par, c_dia],
                scratch=[pltpu.VMEM((span, part), f32)],
            )
            moved_y[dz] = [start(terms[dz][dy], along_y(dy)) for dy in others]

        def add_body(*refs):
            refs[-1][...] = sum(ref[...].astype(f32) for ref in refs[:-1]).astype(refs[-1].dtype)

        def add(values, dtype, **options):
            return run("add_blocks", add_body, [(values[0].shape, dtype)], values, **options)[0]

        def sum_body(*refs):
            z, y, core, q = place()
            for out, at in zip(refs[-2:], (aligned(core, rows), aligned(1 - core, rows))):
                out[...] = sum(ref[at, :].astype(f32) for ref in refs[:-2]).astype(bf16)

        def features_of(blocks, full, out):
            total = sum(
                jnp.dot(
                    block, full[dz * span : (dz + 1) * span, :], preferred_element_type=f32
                )
                for block, dz in zip(blocks, g_order)
            )
            out[...] = (total * feat ** (-0.5)).astype(bf16)

        def fill_body(*refs):
            z, y, core, q = place()
            for k in range(nz * ny):
                dz, dy = w_order[k // ny], k % ny
                ref, at = (refs[k], 0) if dz != 1 else (refs[-2], dy * 2 * rows)
                block = (z ^ lax.rem(z + dz, nz)) * ny + lax.rem(y + dy, ny)
                refs[-1][aligned(block, 2 * rows), :] = ref[at : at + 2 * rows, :]

        def near_body(own, sib, full, f_own, f_sib):
            for ref, out in ((own, f_own), (sib, f_sib)):
                features_of([ref[:, k * span : (k + 1) * span] for k in range(nz)], full, out)

        def far_body(*refs):
            features_of([ref[...] for ref in refs[:nz]], refs[nz], refs[nz + 1])

        def far_features(blocks):
            return run(
                "far_features", far_body, [((tokens, part), bf16)], [*blocks, w_full]
            )[0]

        def place_body(*refs):
            z, y, core, q = place()
            for j in range(4):
                refs[4][:, aligned(q ^ j, part)] = refs[j][...]

        w_order = [0, 3, 2, 1]
        others = range(1, ny)
        w_line = [None] * nz
        w_side = [None] * nz
        far_par, far_dia = [None] * nz, [None] * nz
        terms, moved_y = [None] * nz, [None] * nz

        def teacher_y(dz, *gates):
            w_side[dz] = [start(w_line[dz], along_y(-dy), *gates) for dy in others]

        def block_sum(dz, *more, **options):
            return add([terms[dz][0], *moved_y[dz], *more], bf16, **options)

        first, near_own, c_own, *rest = run(
            "cut_tokens",
            cut_body,
            [
                ((tokens, width), bf16)
                for width in (lead + span, feat + part, part, *[span] * (nz - 1))
            ],
            [patches, cotangent],
        )
        message = start(first, partner)
        near_sib = start(near_own, sibling)
        w_same, w_other = run("cast_teacher", cast_body, [((rows, part), bf16)] * 2, [teacher])
        w_sib = start(w_other, sibling)
        (w_line[0],) = run(
            "join_teacher", join_body, [((2 * rows, part), bf16)], [w_same, w_sib]
        )
        w_line[3] = start(w_line[0], along_z(1))
        teacher_y(0)
        w_line[2] = start(w_line[3], along_z(1))
        teacher_y(3, *w_side[0])
        (turn,) = run(
            "stack_teacher", stack_body, [((ny * 2 * rows, part), bf16)], [w_line[0], *w_side[0]]
        )
        turn = start(turn, along_z(-1), w_line[2])
        teacher_y(2)
        for k in range(1, nz):
            far_par[k] = start(rest[k - 1], partner, *far_par[1 : k - 1])
        c_other, c_par, far_par[0] = run(
            "split_message",
            split_body,
            [((tokens, part), bf16)] * 2 + [((tokens, span), bf16)],
            [after(message, near_sib, w_line[2], *w_side[3])],
        )
        c_dia = start(c_other, sibling)
        held = ([], [], w_side[2])
        for k in range(nz - 1):
            far_dia[k] = start(far_par[k], sibling, *held[k])
        gradient_block(0)
        gradient_block(1)
        onward = start(block_sum(3), across_z(1))
        gradient_block(2)
        far_dia[3] = start(far_par[3], sibling, turn, terms[1][0])
        (w_full,) = run(
            "fill_teacher",
            fill_body,
            [((feat, part), bf16)],
            [*(w for dz in w_order[:-1] for w in (w_line[dz], *w_side[dz])), turn],
        )
        onward = start(block_sum(2, onward), across_z(2))
        f_par = start(far_features(far_par), partner)
        gradient_block(3)
        f_dia = start(far_features(far_dia), diagonal)
        back = start(block_sum(1), across_z(1))
        f_own, f_sib = run(
            "near_features",
            near_body,
            [((tokens, part), bf16)] * 2,
            [near_own, near_sib, w_full],
        )
        f_sib = start(f_sib, sibling)
        wait(f_par, f_dia)
        pieces = [terms[0][0], *moved_y[0], onward, back]
        if pair_groups > 1:
            total = add(pieces, f32)
            sent = total.astype(bf16)
            pieces = [total] + [start(sent, along_g(dg)) for dg in range(1, pair_groups)]
        mine, other = run("sum_gradient", sum_body, [((rows, part), bf16)] * 2, pieces)
        g_par, g_dia, g_sib = (
            start(mine, partner), start(other, diagonal), start(other, sibling)
        )
        (features,) = run(
            "place_features",
            place_body,
            [((tokens, outw), bf16)],
            [f_own, f_sib, f_par, f_dia],
        )
        grads = [mine, g_sib, g_par, g_dia]

        def update_body(*refs):
            z, y, core, q = place()
            student, first, second, teach, *outs = refs[4:]
            corr_one = 1.0 - beta_one**STEP
            corr_two = 1.0 - beta_two**STEP
            for j in range(4):
                at = (slice(None), aligned(q ^ j, part))
                gradient = refs[j][...].astype(f32)
                new_first = beta_one * first[at] + (1.0 - beta_one) * gradient
                new_second = beta_two * second[at] + (1.0 - beta_two) * gradient * gradient
                direction = new_first / corr_one / (jnp.sqrt(new_second / corr_two) + adam_eps)
                weights = student[at]
                new_student = weights - learn_rate * (direction + decay_rate * weights)
                outs[0][at] = new_student
                outs[1][at] = new_first
                outs[2][at] = new_second
                outs[3][at] = ema_keep * teach[at] + (1.0 - ema_keep) * new_student

        new = run(
            "update",
            update_body,
            [((rows, outw), f32)] * 4,
            [*grads, student, first_moment, second_moment, teacher],
        )
        return (features, *new)

    tokens_placed, weights_placed = P(("fsdp", "rep"), None), P("fsdp", None)
    return jax.shard_map(
        per_device,
        mesh=mesh,
        in_specs=(tokens_placed,) * 2 + (weights_placed,) * 4,
        out_specs=(tokens_placed,) + (weights_placed,) * 4,
        check_vma=False,
    )
```

```python
import math

import jax
import jax.numpy as jnp
from jax import lax
from jax.experimental import pallas as pl
from jax.experimental.pallas import tpu as pltpu
from jax.sharding import PartitionSpec as P

STEP = 100

beta_one = 0.9
beta_two = 0.999
adam_eps = 1e-08
learn_rate = 0.1
decay_rate = 0.04
ema_keep = 0.994

bf16, f32 = jnp.bfloat16, jnp.float32
VMEM = pl.BlockSpec(memory_space=pltpu.VMEM)
ANY = pl.BlockSpec(memory_space=pl.ANY)


def call(name, body, outs, inputs, scratch=()):
    shapes = [jax.ShapeDtypeStruct(*out) for out in outs]
    moved = sum(a.size * a.dtype.itemsize for a in (*inputs, *shapes))
    held = sum(4 * math.prod(getattr(s, "shape", ())) for s in scratch)
    with jax.named_scope(name):
        return pl.pallas_call(
            body,
            out_shape=shapes,
            in_specs=[VMEM] * len(inputs),
            out_specs=[VMEM] * len(shapes),
            scratch_shapes=list(scratch),
            cost_estimate=pl.CostEstimate(flops=1, bytes_accessed=1, transcendentals=0),
            compiler_params=pltpu.CompilerParams(vmem_limit_bytes=moved + held + 4 * 2**20),
        )(*inputs)


def after(value, *others):
    return lax.optimization_barrier((value, *others))[0]


def aligned(index, size):
    return pl.ds(pl.multiple_of(index * size, size), size)


def solution(mesh):
    n, r = mesh.shape["fsdp"], mesh.shape["rep"]
    nz = 4
    ny = n // (2 * nz)
    pair_groups = r // 2

    def send(value, move):
        perm = []
        for f in range(n):
            for p in range(r):
                z, y, c = f // (2 * ny), f // 2 % ny, f % 2
                z, y, c, g, h = move(z, y, c, p // 2, p % 2)
                perm.append((f * r + p, ((z * ny + y) * 2 + c) * r + g * 2 + h))
        return lax.ppermute(value, ("fsdp", "rep"), perm)

    def sibling(z, y, c, g, h):
        return z, y, 1 - c, g, h

    def partner(z, y, c, g, h):
        return z, y, c, g, 1 - h

    def diagonal(z, y, c, g, h):
        return z, y, 1 - c, g, 1 - h

    def turned(z, d):
        p = ((z ^ (z >> 1)) + d) & 3
        return p ^ (p >> 1)

    def along_z(d):
        return lambda z, y, c, g, h: (turned(z, d), y, c, g, h)

    def across_z(d):
        return lambda z, y, c, g, h: (z ^ d, y, c, g, h)

    def along_y(d):
        return lambda z, y, c, g, h: (z, (y + d) % ny, c, g, h)

    def along_g(d):
        return lambda z, y, c, g, h: (z, y, c, (g + d) % pair_groups, h)

    def place():
        f = lax.axis_index("fsdp")
        core = lax.rem(f, 2)
        return f // (2 * ny), lax.rem(f // 2, ny), core, lax.rem(lax.axis_index("rep"), 2) * 2 + core

    def per_device(patches, cotangent, student, first_moment, second_moment, teacher):
        tokens, feat = patches.shape
        outw = cotangent.shape[1]
        rows = teacher.shape[0]
        part = outw // 4
        span = feat // nz
        g_order = [3, 2, 1, 0]
        lead = 2 * part

        def cut_body(p, c, first, near, c_own, second, third):
            z, y, core, q = place()
            first[:, :lead] = c[:, aligned(1 - q // 2, lead)]
            for k, dz in enumerate(g_order):
                block = p[:, aligned(z ^ dz, span)]
                near[:, k * span : (k + 1) * span] = block
                if k == 0:
                    first[:, lead:] = block
                elif k < 3:
                    second[:, (k - 1) * span : k * span] = block
                else:
                    third[...] = block
            near[:, feat:] = c[:, aligned(q ^ 1, part)]
            c_own[...] = c[:, aligned(q, part)]

        def split_body(message, c_sib, c_here, block):
            z, y, core, q = place()
            c_sib[...] = message[:, aligned(1 - core, part)]
            c_here[...] = message[:, aligned(core, part)]
            block[...] = message[:, lead:]

        def halve_body(message, *blocks):
            for k, out in enumerate(blocks):
                out[...] = message[:, k * span : (k + 1) * span]

        clock = []

        def run(name, body, outs, inputs, *scratch, **options):
            first = after(inputs[0], *clock) if clock else inputs[0]
            out = call(name, body, outs, [first, *inputs[1:]], *scratch, **options)
            clock[:] = out[:1]
            return out

        def start(value, move, *others):
            return send(after(value, *others) if others else value, move)

        def wait(*values):
            clock.extend(values)

        def cast_body(t, same, other):
            z, y, core, q = place()
            same[...] = t[:, aligned(q, part)].astype(bf16)
            other[...] = t[:, aligned(q ^ 1, part)].astype(bf16)

        def join_body(same, sib, out):
            z, y, core, q = place()
            out[aligned(core, rows), :] = same[...]
            out[aligned(1 - core, rows), :] = sib[...]

        def stack_body(*refs):
            for k, ref in enumerate(refs[:-1]):
                refs[-1][k * 2 * rows : (k + 1) * 2 * rows, :] = ref[...]

        def terms_body(k):
            def body(own, sib, par, dia, c0, c_par, c_dia, *outs):
                z, y, core, q = place()
                whole = outs[-1]
                near = slice(k * span, (k + 1) * span)
                total = None
                for p, c in (
                    (own[:, near], c0[...]),
                    (sib[:, near], sib[:, feat:]),
                    (par[...], c_par[...]),
                    (dia[...], c_dia[...]),
                ):
                    term = lax.dot_general(
                        p, c, (((0,), (0,)), ((), ())), preferred_element_type=f32
                    )
                    total = term if total is None else total + term
                whole[...] = total
                for dy in range(ny):
                    block = whole[aligned(lax.rem(y + dy, ny), 2 * rows), :]
                    outs[dy][: 2 * rows, :] = block.astype(outs[dy].dtype)
                    if outs[dy].shape[0] > 2 * rows:
                        rest = (outs[dy].shape[0] - 2 * rows, part)
                        outs[dy][2 * rows :, :] = jnp.zeros(rest, outs[dy].dtype)

            return body

        def gradient_block(k):
            dz = g_order[k]
            terms[dz] = run(
                "gradient_block",
                terms_body(k),
                [((2 * rows, part), f32)] + [((2 * rows + 16 * (k == 0), part), bf16)] * (ny - 1),
                [near_own, near_sib, far_par[k], far_dia[k], c_own, c_par, c_dia],
                scratch=[pltpu.VMEM((span, part), f32)],
            )
            gates = () if k else w_side[2]
            moved_y[dz] = [start(terms[dz][dy], along_y(dy), *gates) for dy in others]

        def add_body(*refs):
            count = refs[-1].shape[0]
            total = sum(ref[:count, :].astype(f32) for ref in refs[:-1])
            refs[-1][...] = total.astype(refs[-1].dtype)

        def add(values, dtype, **options):
            return run("add_blocks", add_body, [(values[0].shape, dtype)], values, **options)[0]

        def sum_body(*refs):
            z, y, core, q = place()
            for out, at in zip(refs[-2:], (aligned(core, rows), aligned(1 - core, rows))):
                out[...] = sum(ref[at, :].astype(f32) for ref in refs[:-2]).astype(bf16)

        def features_of(blocks, full, out):
            total = sum(
                jnp.dot(
                    block, full[dz * span : (dz + 1) * span, :], preferred_element_type=f32
                )
                for block, dz in zip(blocks, g_order)
            )
            out[...] = (total * feat ** (-0.5)).astype(bf16)

        def fill_body(*refs):
            z, y, core, q = place()
            for k in range(nz * ny):
                dz, dy = w_order[k // ny], k % ny
                ref, at = (refs[k], 0) if dz != 1 else (refs[-2], dy * 2 * rows)
                block = (z ^ turned(z, dz)) * ny + lax.rem(y + dy, ny)
                refs[-1][aligned(block, 2 * rows), :] = ref[at : at + 2 * rows, :]

        def near_body(own, sib, full, f_own, f_sib):
            for ref, out in ((own, f_own), (sib, f_sib)):
                features_of([ref[:, k * span : (k + 1) * span] for k in range(nz)], full, out)

        def far_body(*refs):
            features_of([ref[...] for ref in refs[:nz]], refs[nz], refs[nz + 1])

        def far_features(blocks):
            return run(
                "far_features", far_body, [((tokens, part), bf16)], [*blocks, w_full]
            )[0]

        def place_body(*refs):
            z, y, core, q = place()
            for j in range(4):
                refs[4][:, aligned(q ^ j, part)] = refs[j][...]

        w_order = [0, 3, 2, 1]
        others = range(1, ny)
        w_line = [None] * nz
        w_side = [None] * nz
        far_par, far_dia = [None] * nz, [None] * nz
        terms, moved_y = [None] * nz, [None] * nz

        def teacher_y(dz, *gates):
            w_side[dz] = [start(w_line[dz], along_y(-dy), *gates) for dy in others]

        def block_sum(dz, *more, **options):
            return add([terms[dz][0], *moved_y[dz], *more], bf16, **options)

        first, near_own, c_own, second, third = run(
            "cut_tokens",
            cut_body,
            [
                ((tokens, width), bf16)
                for width in (lead + span, feat + part, part, 2 * span, span)
            ],
            [patches, cotangent],
        )
        message = start(first, partner)
        near_sib = start(near_own, sibling)
        w_same, w_other = run("cast_teacher", cast_body, [((rows, part), bf16)] * 2, [after(teacher, first)])
        w_sib = start(w_other, sibling)
        (w_line[0],) = run(
            "join_teacher", join_body, [((2 * rows, part), bf16)], [w_same, w_sib]
        )
        w_line[3] = start(w_line[0], along_z(1))
        teacher_y(0)
        w_line[2] = start(w_line[3], along_z(1))
        teacher_y(3, *w_side[0])
        (turn,) = run(
            "stack_teacher", stack_body, [((ny * 2 * rows, part), bf16)], [w_line[0], *w_side[0]]
        )
        teacher_y(2)
        second = start(second, partner)
        c_other, c_par, far_par[0] = run(
            "split_message",
            split_body,
            [((tokens, part), bf16)] * 2 + [((tokens, span), bf16)],
            [after(message, near_sib, w_line[2], *w_side[3])],
        )
        c_dia = start(c_other, sibling)
        far_dia[0] = start(far_par[0], sibling)
        gradient_block(0)
        begun = terms[3][0]
        far_par[3] = start(third, partner, begun)
        turn = start(turn, along_z(-1), begun)
        far_par[1:3] = run(
            "halve_message", halve_body, [((tokens, span), bf16)] * 2, [second]
        )
        far_dia[1] = start(far_par[1], sibling)
        gradient_block(1)
        onward = start(block_sum(3), across_z(1))
        far_dia[2] = start(far_par[2], sibling)
        gradient_block(2)
        far_dia[3] = start(far_par[3], sibling, turn, terms[1][0])
        (w_full,) = run(
            "fill_teacher",
            fill_body,
            [((feat, part), bf16)],
            [*(w for dz in w_order[:-1] for w in (w_line[dz], *w_side[dz])), turn],
        )
        f_par = start(far_features(far_par), partner)
        onward = start(block_sum(2, onward), across_z(2))
        gradient_block(3)
        f_dia = start(far_features(far_dia), diagonal)
        back = start(block_sum(1), across_z(1))
        f_own, f_sib = run(
            "near_features",
            near_body,
            [((tokens, part), bf16)] * 2,
            [near_own, near_sib, w_full],
        )
        f_sib = start(f_sib, sibling)
        wait(f_par, f_dia)
        pieces = [terms[0][0], *moved_y[0], onward, back]
        if pair_groups > 1:
            total = add(pieces, f32)
            sent = total.astype(bf16)
            pieces = [total] + [start(sent, along_g(dg)) for dg in range(1, pair_groups)]
        mine, other = run("sum_gradient", sum_body, [((rows, part), bf16)] * 2, pieces)
        g_par, g_dia, g_sib = (
            start(mine, partner), start(other, diagonal), start(other, sibling)
        )
        def update_body(quarters):
            def body(*refs):
                z, y, core, q = place()
                student, first, second, teach = refs[2:6]
                outs, held, sems = refs[-6:-2], refs[-2], refs[-1]
                corr_one = 1.0 - beta_one**STEP
                corr_two = 1.0 - beta_two**STEP
                copies = []
                for i, j in enumerate(quarters):
                    at = (slice(None), aligned(q ^ j, part))
                    gradient = refs[i][...].astype(f32)
                    new_first = beta_one * first[at] + (1.0 - beta_one) * gradient
                    new_second = beta_two * second[at] + (1.0 - beta_two) * gradient * gradient
                    direction = new_first / corr_one / (jnp.sqrt(new_second / corr_two) + adam_eps)
                    weights = student[at]
                    new_student = weights - learn_rate * (direction + decay_rate * weights)
                    new_teacher = ema_keep * teach[at] + (1.0 - ema_keep) * new_student
                    for k, new in enumerate((new_student, new_first, new_second, new_teacher)):
                        held[4 * i + k] = new
                        copies.append(
                            pltpu.make_async_copy(
                                held.at[4 * i + k], outs[k].at[at], sems.at[4 * i + k]
                            )
                        )
                        copies[-1].start()
                for copy in copies:
                    copy.wait()

            return body

        def update(name, quarters, grads, begun):
            inputs = [after(grads[0], *clock), *grads[1:]]
            inputs += [student, first_moment, second_moment, teacher]
            with jax.named_scope(name):
                out = pl.pallas_call(
                    update_body(quarters),
                    out_shape=[jax.ShapeDtypeStruct((rows, outw), f32)] * 4,
                    in_specs=[VMEM] * 6 + [ANY] * len(begun),
                    out_specs=[ANY] * 4,
                    input_output_aliases={6 + k: k for k in range(len(begun))},
                    scratch_shapes=[
                        pltpu.VMEM((8, rows, part), f32), pltpu.SemaphoreType.DMA((8,))
                    ],
                    cost_estimate=pl.CostEstimate(flops=1, bytes_accessed=1, transcendentals=0),
                    compiler_params=pltpu.CompilerParams(vmem_limit_bytes=16 * 2**20),
                )(*inputs, *begun)
            clock[:] = out[:1]
            return out

        new = update("update_near", (0, 1), [mine, g_sib], [])
        (features,) = run(
            "place_features",
            place_body,
            [((tokens, outw), bf16)],
            [f_own, f_sib, f_par, f_dia],
        )
        new = update("update_far", (2, 3), [g_par, g_dia], new)
        return (features, *new)

    tokens_placed, weights_placed = P(("fsdp", "rep"), None), P("fsdp", None)
    return jax.shard_map(
        per_device,
        mesh=mesh,
        in_specs=(tokens_placed,) * 2 + (weights_placed,) * 4,
        out_specs=(tokens_placed,) + (weights_placed,) * 4,
        check_vma=False,
    )
```

```python
import math

import jax
import jax.numpy as jnp
from jax import lax
from jax.experimental import pallas as pl
from jax.experimental.pallas import tpu as pltpu
from jax.sharding import PartitionSpec as P

STEP = 100

beta_one = 0.9
beta_two = 0.999
adam_eps = 1e-08
learn_rate = 0.1
decay_rate = 0.04
ema_keep = 0.994

bf16, f32 = jnp.bfloat16, jnp.float32
VMEM = pl.BlockSpec(memory_space=pltpu.VMEM)
ANY = pl.BlockSpec(memory_space=pl.ANY)


def call(name, body, outs, inputs, scratch=()):
    shapes = [jax.ShapeDtypeStruct(*out) for out in outs]
    moved = sum(a.size * a.dtype.itemsize for a in (*inputs, *shapes))
    held = sum(4 * math.prod(getattr(s, "shape", ())) for s in scratch)
    with jax.named_scope(name):
        return pl.pallas_call(
            body,
            out_shape=shapes,
            in_specs=[VMEM] * len(inputs),
            out_specs=[VMEM] * len(shapes),
            scratch_shapes=list(scratch),
            cost_estimate=pl.CostEstimate(flops=1, bytes_accessed=1, transcendentals=0),
            compiler_params=pltpu.CompilerParams(vmem_limit_bytes=moved + held + 4 * 2**20),
        )(*inputs)


def after(value, *others):
    return lax.optimization_barrier((value, *others))[0]


def aligned(index, size):
    return pl.ds(pl.multiple_of(index * size, size), size)


def solution(mesh):
    n, r = mesh.shape["fsdp"], mesh.shape["rep"]
    nz = 4
    ny = n // (2 * nz)
    pair_groups = r // 2

    def send(value, move):
        perm = []
        for f in range(n):
            for p in range(r):
                z, y, c = f // (2 * ny), f // 2 % ny, f % 2
                z, y, c, g, h = move(z, y, c, p // 2, p % 2)
                perm.append((f * r + p, ((z * ny + y) * 2 + c) * r + g * 2 + h))
        return lax.ppermute(value, ("fsdp", "rep"), perm)

    def sibling(z, y, c, g, h):
        return z, y, 1 - c, g, h

    def partner(z, y, c, g, h):
        return z, y, c, g, 1 - h

    def diagonal(z, y, c, g, h):
        return z, y, 1 - c, g, 1 - h

    def turned(z, d):
        p = ((z ^ (z >> 1)) + d) & 3
        return p ^ (p >> 1)

    def along_z(d):
        return lambda z, y, c, g, h: (turned(z, d), y, c, g, h)

    def across_z(d):
        return lambda z, y, c, g, h: (z ^ d, y, c, g, h)

    def along_y(d):
        return lambda z, y, c, g, h: (z, (y + d) % ny, c, g, h)

    def along_g(d):
        return lambda z, y, c, g, h: (z, y, c, (g + d) % pair_groups, h)

    def place():
        f = lax.axis_index("fsdp")
        core = lax.rem(f, 2)
        return f // (2 * ny), lax.rem(f // 2, ny), core, lax.rem(lax.axis_index("rep"), 2) * 2 + core

    def per_device(patches, cotangent, student, first_moment, second_moment, teacher):
        tokens, feat = patches.shape
        outw = cotangent.shape[1]
        rows = teacher.shape[0]
        part = outw // 4
        span = feat // nz
        g_order = [3, 2, 1, 0]
        lead = 2 * part
        extra = 16

        def cut_body(p, c, first, near, c_own, second, third, mark):
            z, y, core, q = place()
            mark[...] = c[: mark.shape[0], :part]
            first[:, :lead] = c[:, aligned(1 - q // 2, lead)]
            for k, dz in enumerate(g_order):
                block = p[:, aligned(z ^ dz, span)]
                near[:, k * span : (k + 1) * span] = block
                if k == 0:
                    first[:, lead:] = block
                elif k == 1:
                    second[:tokens, :] = block
                    second[tokens:, :] = block[: second.shape[0] - tokens, :]
                else:
                    third[:, (k - 2) * span : (k - 1) * span] = block
            near[:, feat:] = c[:, aligned(q ^ 1, part)]
            c_own[...] = c[:, aligned(q, part)]

        def split_body(message, c_sib, c_here, block):
            z, y, core, q = place()
            c_sib[...] = message[:, aligned(1 - core, part)]
            c_here[...] = message[:, aligned(core, part)]
            block[...] = message[:, lead:]

        def halve_body(message, *blocks):
            for k, out in enumerate(blocks):
                out[...] = message[:tokens, k * span : (k + 1) * span]

        clock = []

        def run(name, body, outs, inputs, *scratch, **options):
            first = after(inputs[0], *clock) if clock else inputs[0]
            out = call(name, body, outs, [first, *inputs[1:]], *scratch, **options)
            clock[:] = out[:1]
            return out

        def start(value, move, *others):
            return send(after(value, *others) if others else value, move)

        def wait(*values):
            clock.extend(values)

        def cast_body(t, same, other):
            z, y, core, q = place()
            same[...] = t[:, aligned(q, part)].astype(bf16)
            other[...] = t[:, aligned(q ^ 1, part)].astype(bf16)

        def join_body(same, sib, out):
            z, y, core, q = place()
            out[aligned(core, rows), :] = same[...]
            out[aligned(1 - core, rows), :] = sib[...]

        def stack_body(*refs):
            for k, ref in enumerate(refs[:-1]):
                refs[-1][k * 2 * rows : (k + 1) * 2 * rows, :] = ref[...]
            refs[-1][ny * 2 * rows :, :] = refs[0][: 2 * extra, :]

        def terms_body(k):
            def body(own, sib, par, dia, c0, c_par, c_dia, *outs):
                z, y, core, q = place()
                whole = outs[-1]
                near = slice(k * span, (k + 1) * span)
                total = None
                for p, c in (
                    (own[:, near], c0[...]),
                    (sib[:, near], sib[:, feat:]),
                    (par[...], c_par[...]),
                    (dia[...], c_dia[...]),
                ):
                    term = lax.dot_general(
                        p, c, (((0,), (0,)), ((), ())), preferred_element_type=f32
                    )
                    total = term if total is None else total + term
                whole[...] = total
                for dy in range(ny):
                    block = whole[aligned(lax.rem(y + dy, ny), 2 * rows), :]
                    outs[dy][: 2 * rows, :] = block.astype(outs[dy].dtype)
                    if outs[dy].shape[0] > 2 * rows:
                        rest = (outs[dy].shape[0] - 2 * rows, part)
                        outs[dy][2 * rows :, :] = jnp.zeros(rest, outs[dy].dtype)

            return body

        def gradient_block(k):
            dz = g_order[k]
            terms[dz] = run(
                "gradient_block",
                terms_body(k),
                [((2 * rows, part), f32)]
                + [((2 * rows + (extra, 2 * extra, 0, 0)[k], part), bf16)] * (ny - 1),
                [near_own, near_sib, far_par[k], far_dia[k], c_own, c_par, c_dia],
                scratch=[pltpu.VMEM((span, part), f32)],
            )
            moved_y[dz] = [start(terms[dz][dy], along_y(dy)) for dy in others]

        def add_body(*refs):
            total = sum(ref[: 2 * rows, :].astype(f32) for ref in refs[:-1])
            refs[-1][: 2 * rows, :] = total.astype(refs[-1].dtype)
            if refs[-1].shape[0] > 2 * rows:
                rest = (refs[-1].shape[0] - 2 * rows, part)
                refs[-1][2 * rows :, :] = jnp.zeros(rest, refs[-1].dtype)

        def add(values, dtype, more=0):
            return run("add_blocks", add_body, [((2 * rows + more, part), dtype)], values)[0]

        def sum_body(*refs):
            z, y, core, q = place()
            for out, at in zip(refs[-2:], (aligned(core, rows), aligned(1 - core, rows))):
                out[...] = sum(ref[at, :].astype(f32) for ref in refs[:-3]).astype(bf16)

        def features_of(blocks, full, out):
            total = sum(
                jnp.dot(
                    block, full[dz * span : (dz + 1) * span, :], preferred_element_type=f32
                )
                for block, dz in zip(blocks, g_order)
            )
            out[...] = (total * feat ** (-0.5)).astype(bf16)

        def fill_body(*refs):
            z, y, core, q = place()
            for k in range(nz * ny):
                dz, dy = w_order[k // ny], k % ny
                ref, at = (refs[k], 0) if dz != 1 else (refs[-2], dy * 2 * rows)
                block = (z ^ turned(z, dz)) * ny + lax.rem(y + dy, ny)
                refs[-1][aligned(block, 2 * rows), :] = ref[at : at + 2 * rows, :]

        def near_body(own, sib, full, f_own, f_sib):
            for ref, out in ((own, f_own), (sib, f_sib)):
                features_of([ref[:, k * span : (k + 1) * span] for k in range(nz)], full, out)

        def far_body(*refs):
            features_of([ref[...] for ref in refs[:nz]], refs[nz], refs[nz + 1])

        def far_features(blocks):
            return run(
                "far_features", far_body, [((tokens, part), bf16)], [*blocks, w_full]
            )[0]

        def place_body(*refs):
            z, y, core, q = place()
            for j in range(4):
                refs[4][:, aligned(q ^ j, part)] = refs[j][...]

        w_order = [0, 3, 2, 1]
        others = range(1, ny)
        w_line = [None] * nz
        w_side = [None] * nz
        far_par, far_dia = [None] * nz, [None] * nz
        terms, moved_y = [None] * nz, [None] * nz

        def teacher_y(dz, *gates):
            w_side[dz] = [start(w_line[dz], along_y(-dy), *gates) for dy in others]

        def block_sum(dz, *parts, more=0):
            return add([terms[dz][0], *moved_y[dz], *parts], bf16, more)

        first, near_own, c_own, second, third, mark = run(
            "cut_tokens",
            cut_body,
            [
                ((count, width), bf16)
                for count, width in (
                    (tokens, lead + span), (tokens, feat + part), (tokens, part),
                    (tokens + 2 * extra, span), (tokens, 2 * span), (tokens - extra, part),
                )
            ],
            [patches, cotangent],
        )
        message = start(first, partner)
        near_sib = start(near_own, sibling)
        w_same, w_other = run("cast_teacher", cast_body, [((rows, part), bf16)] * 2, [after(teacher, first)])
        w_sib = start(w_other, sibling)
        (w_line[0],) = run(
            "join_teacher", join_body, [((2 * rows, part), bf16)], [w_same, w_sib]
        )
        w_line[3] = start(w_line[0], along_z(1))
        teacher_y(0)
        teacher_y(3, *w_side[0])
        (turn,) = run(
            "stack_teacher",
            stack_body,
            [((ny * 2 * rows + 2 * extra, part), bf16)],
            [after(w_line[0], near_sib), *w_side[0]],
        )
        turn = start(turn, along_z(-1))
        w_line[2] = start(w_line[3], along_z(1), turn)
        block = start(second, partner)
        c_other, c_par, far_par[0] = run(
            "split_message",
            split_body,
            [((tokens, part), bf16)] * 2 + [((tokens, span), bf16)],
            [after(message, near_sib, *w_side[3])],
        )
        c_dia = start(c_other, sibling)
        far_dia[0] = start(far_par[0], sibling)
        gradient_block(0)
        both = start(third, partner)
        (far_par[1],) = run("take_block", halve_body, [((tokens, span), bf16)], [block])
        far_dia[1] = start(far_par[1], sibling)
        wait(turn)
        gradient_block(1)
        onward = block_sum(3, more=2 * extra)
        teacher_y(2, onward)
        onward = start(onward, across_z(1))
        far_par[2:] = run(
            "halve_message", halve_body, [((tokens, span), bf16)] * 2, [after(both, w_line[2])]
        )
        far_dia[2] = start(far_par[2], sibling)
        gradient_block(2)
        onward = start(block_sum(2, onward), across_z(2))
        far_dia[3] = start(far_par[3], sibling, terms[1][0])
        (w_full,) = run(
            "fill_teacher",
            fill_body,
            [((feat, part), bf16)],
            [*(w for dz in w_order[:-1] for w in (w_line[dz], *w_side[dz])), turn],
        )
        f_par = start(far_features(far_par), partner)
        gradient_block(3)
        f_dia = start(far_features(far_dia), diagonal)
        back = start(block_sum(1), across_z(1))
        f_own, f_sib = run(
            "near_features",
            near_body,
            [((tokens, part), bf16)] * 2,
            [near_own, near_sib, w_full],
        )
        f_sib = start(f_sib, sibling)
        wait(f_par, f_dia)
        pieces = [terms[0][0], *moved_y[0], onward, back]
        spacer = start(mark, sibling, onward)
        if pair_groups > 1:
            total = add(pieces, f32)
            sent = total.astype(bf16)
            pieces = [total] + [start(sent, along_g(dg)) for dg in range(1, pair_groups)]
        mine, other = run("sum_gradient", sum_body, [((rows, part), bf16)] * 2, [*pieces, spacer])
        g_par, g_dia, g_sib = (
            start(mine, partner), start(other, diagonal), start(other, sibling)
        )
        def update_body(quarters):
            def body(*refs):
                z, y, core, q = place()
                student, first, second, teach = refs[2:6]
                outs, held, sems = refs[-6:-2], refs[-2], refs[-1]
                corr_one = 1.0 - beta_one**STEP
                corr_two = 1.0 - beta_two**STEP
                copies = []
                for i, j in enumerate(quarters):
                    at = (slice(None), aligned(q ^ j, part))
                    gradient = refs[i][...].astype(f32)
                    new_first = beta_one * first[at] + (1.0 - beta_one) * gradient
                    new_second = beta_two * second[at] + (1.0 - beta_two) * gradient * gradient
                    direction = new_first / corr_one / (jnp.sqrt(new_second / corr_two) + adam_eps)
                    weights = student[at]
                    new_student = weights - learn_rate * (direction + decay_rate * weights)
                    new_teacher = ema_keep * teach[at] + (1.0 - ema_keep) * new_student
                    for k, new in enumerate((new_student, new_first, new_second, new_teacher)):
                        held[4 * i + k] = new
                        copies.append(
                            pltpu.make_async_copy(
                                held.at[4 * i + k], outs[k].at[at], sems.at[4 * i + k]
                            )
                        )
                        copies[-1].start()
                for copy in copies:
                    copy.wait()

            return body

        def update(name, quarters, grads, begun):
            inputs = [after(grads[0], *clock), *grads[1:]]
            inputs += [student, first_moment, second_moment, teacher]
            with jax.named_scope(name):
                out = pl.pallas_call(
                    update_body(quarters),
                    out_shape=[jax.ShapeDtypeStruct((rows, outw), f32)] * 4,
                    in_specs=[VMEM] * 6 + [ANY] * len(begun),
                    out_specs=[ANY] * 4,
                    input_output_aliases={6 + k: k for k in range(len(begun))},
                    scratch_shapes=[
                        pltpu.VMEM((8, rows, part), f32), pltpu.SemaphoreType.DMA((8,))
                    ],
                    cost_estimate=pl.CostEstimate(flops=1, bytes_accessed=1, transcendentals=0),
                    compiler_params=pltpu.CompilerParams(vmem_limit_bytes=16 * 2**20),
                )(*inputs, *begun)
            clock[:] = out[:1]
            return out

        new = update("update_near", (0, 1), [mine, g_sib], [])
        (features,) = run(
            "place_features",
            place_body,
            [((tokens, outw), bf16)],
            [f_own, f_sib, f_par, f_dia],
        )
        new = update("update_far", (2, 3), [g_par, g_dia], new)
        return (features, *new)

    tokens_placed, weights_placed = P(("fsdp", "rep"), None), P("fsdp", None)
    return jax.shard_map(
        per_device,
        mesh=mesh,
        in_specs=(tokens_placed,) * 2 + (weights_placed,) * 4,
        out_specs=(tokens_placed,) + (weights_placed,) * 4,
        check_vma=False,
    )
```

```python
import math

import jax
import jax.numpy as jnp
from jax import lax
from jax.experimental import pallas as pl
from jax.experimental.pallas import tpu as pltpu
from jax.sharding import PartitionSpec as P

STEP = 100

beta_one = 0.9
beta_two = 0.999
adam_eps = 1e-08
learn_rate = 0.1
decay_rate = 0.04
ema_keep = 0.994

bf16, f32 = jnp.bfloat16, jnp.float32
VMEM = pl.BlockSpec(memory_space=pltpu.VMEM)
ANY = pl.BlockSpec(memory_space=pl.ANY)


def call(name, body, outs, inputs, scratch=()):
    shapes = [jax.ShapeDtypeStruct(*out) for out in outs]
    moved = sum(a.size * a.dtype.itemsize for a in (*inputs, *shapes))
    held = sum(4 * math.prod(getattr(s, "shape", ())) for s in scratch)
    with jax.named_scope(name):
        return pl.pallas_call(
            body,
            out_shape=shapes,
            in_specs=[VMEM] * len(inputs),
            out_specs=[VMEM] * len(shapes),
            scratch_shapes=list(scratch),
            cost_estimate=pl.CostEstimate(flops=1, bytes_accessed=1, transcendentals=0),
            compiler_params=pltpu.CompilerParams(vmem_limit_bytes=moved + held + 4 * 2**20),
        )(*inputs)


def after(value, *others):
    return lax.optimization_barrier((value, *others))[0]


def aligned(index, size):
    return pl.ds(pl.multiple_of(index * size, size), size)


def solution(mesh):
    n, r = mesh.shape["fsdp"], mesh.shape["rep"]
    nz = 4
    ny = n // (2 * nz)
    pair_groups = r // 2

    def send(value, move):
        perm = []
        for f in range(n):
            for p in range(r):
                z, y, c = f // (2 * ny), f // 2 % ny, f % 2
                z, y, c, g, h = move(z, y, c, p // 2, p % 2)
                perm.append((f * r + p, ((z * ny + y) * 2 + c) * r + g * 2 + h))
        return lax.ppermute(value, ("fsdp", "rep"), perm)

    def sibling(z, y, c, g, h):
        return z, y, 1 - c, g, h

    def partner(z, y, c, g, h):
        return z, y, c, g, 1 - h

    def diagonal(z, y, c, g, h):
        return z, y, 1 - c, g, 1 - h

    def turned(z, d):
        p = ((z ^ (z >> 1)) + d) & 3
        return p ^ (p >> 1)

    def along_z(d):
        return lambda z, y, c, g, h: (turned(z, d), y, c, g, h)

    def across_z(d):
        return lambda z, y, c, g, h: (z ^ d, y, c, g, h)

    def along_y(d):
        return lambda z, y, c, g, h: (z, (y + d) % ny, c, g, h)

    def along_g(d):
        return lambda z, y, c, g, h: (z, y, c, (g + d) % pair_groups, h)

    def place():
        f = lax.axis_index("fsdp")
        core = lax.rem(f, 2)
        return f // (2 * ny), lax.rem(f // 2, ny), core, lax.rem(lax.axis_index("rep"), 2) * 2 + core

    def per_device(patches, cotangent, student, first_moment, second_moment, teacher):
        tokens, feat = patches.shape
        outw = cotangent.shape[1]
        rows = teacher.shape[0]
        part = outw // 4
        span = feat // nz
        g_order = [3, 2, 1, 0]
        lead = 2 * part
        extra = 16

        def cut_body(p, c, first, near, c_own, second, third, mark):
            z, y, core, q = place()
            mark[...] = c[: mark.shape[0], :part]
            first[:, :lead] = c[:, aligned(1 - q // 2, lead)]
            for k, dz in enumerate(g_order):
                block = p[:, aligned(z ^ dz, span)]
                near[:, k * span : (k + 1) * span] = block
                if k == 0:
                    first[:, lead:] = block
                elif k == 1:
                    second[:tokens, :] = block
                    second[tokens:, :] = block[: second.shape[0] - tokens, :]
                else:
                    third[:, (k - 2) * span : (k - 1) * span] = block
            near[:, feat:] = c[:, aligned(q ^ 1, part)]
            c_own[...] = c[:, aligned(q, part)]

        def split_body(message, c_sib, c_here, block):
            z, y, core, q = place()
            c_sib[...] = message[:, aligned(1 - core, part)]
            c_here[...] = message[:, aligned(core, part)]
            block[...] = message[:, lead:]

        def first_body(message, block):
            block[...] = message[:tokens, :]

        def take_body(message, upper, lower, first, second):
            first[...] = message[:, :span]
            second[...] = message[:, span:]
            upper[...] = message[: tokens // 2, :span]
            lower[...] = message[tokens // 2 :, :span]

        def pieces_body(upper, lower, block):
            block[: tokens // 2, :] = upper[...]
            block[tokens // 2 :, :] = lower[...]

        clock = []

        def run(name, body, outs, inputs, *scratch, **options):
            first = after(inputs[0], *clock) if clock else inputs[0]
            out = call(name, body, outs, [first, *inputs[1:]], *scratch, **options)
            clock[:] = out[:1]
            return out

        def start(value, move, *others):
            return send(after(value, *others) if others else value, move)

        def wait(*values):
            clock.extend(values)

        def cast_body(t, same, other):
            z, y, core, q = place()
            same[...] = t[:, aligned(q, part)].astype(bf16)
            other[:rows, :] = t[:, aligned(q ^ 1, part)].astype(bf16)
            other[rows:, :] = jnp.zeros((other.shape[0] - rows, part), bf16)

        def join_body(same, sib, out):
            z, y, core, q = place()
            out[aligned(core, rows), :] = same[...]
            out[aligned(1 - core, rows), :] = sib[:rows, :]

        def stack_body(*refs):
            for k, ref in enumerate(refs[:-1]):
                refs[-1][k * 2 * rows : (k + 1) * 2 * rows, :] = ref[...]
            refs[-1][ny * 2 * rows :, :] = refs[0][: 2 * extra, :]

        def terms_body(k):
            def body(own, sib, par, dia, c0, c_par, c_dia, *outs):
                z, y, core, q = place()
                whole = outs[-1]
                near = slice(k * span, (k + 1) * span)
                total = None
                for p, c in (
                    (own[:, near], c0[...]),
                    (sib[:, near], sib[:, feat:]),
                    (par[...], c_par[...]),
                    (dia[...], c_dia[...]),
                ):
                    term = lax.dot_general(
                        p, c, (((0,), (0,)), ((), ())), preferred_element_type=f32
                    )
                    total = term if total is None else total + term
                whole[...] = total
                for dy in range(ny):
                    block = whole[aligned(lax.rem(y + dy, ny), 2 * rows), :]
                    outs[dy][: 2 * rows, :] = block.astype(outs[dy].dtype)
                    if outs[dy].shape[0] > 2 * rows:
                        rest = (outs[dy].shape[0] - 2 * rows, part)
                        outs[dy][2 * rows :, :] = jnp.zeros(rest, outs[dy].dtype)

            return body

        def gradient_block(k):
            dz = g_order[k]
            terms[dz] = run(
                "gradient_block",
                terms_body(k),
                [((2 * rows, part), f32)]
                + [((2 * rows + extra * (k == 0), part), bf16)] * (ny - 1),
                [near_own, near_sib, far_par[k], far_dia[k], c_own, c_par, c_dia],
                scratch=[pltpu.VMEM((span, part), f32)],
            )
            moved_y[dz] = [start(terms[dz][dy], along_y(dy)) for dy in others]

        def add_body(*refs):
            total = sum(ref[: 2 * rows, :].astype(f32) for ref in refs[:-1])
            refs[-1][: 2 * rows, :] = total.astype(refs[-1].dtype)
            if refs[-1].shape[0] > 2 * rows:
                rest = (refs[-1].shape[0] - 2 * rows, part)
                refs[-1][2 * rows :, :] = jnp.zeros(rest, refs[-1].dtype)

        def add(values, dtype, more=0):
            return run("add_blocks", add_body, [((2 * rows + more, part), dtype)], values)[0]

        def sum_body(*refs):
            z, y, core, q = place()
            for out, at in zip(refs[-2:], (aligned(core, rows), aligned(1 - core, rows))):
                out[...] = sum(ref[at, :].astype(f32) for ref in refs[:-3]).astype(bf16)

        def features_of(blocks, full, out):
            total = sum(
                jnp.dot(
                    block, full[dz * span : (dz + 1) * span, :], preferred_element_type=f32
                )
                for block, dz in zip(blocks, g_order)
            )
            out[...] = (total * feat ** (-0.5)).astype(bf16)

        def fill_body(*refs):
            z, y, core, q = place()
            for k in range(nz * ny):
                dz, dy = w_order[k // ny], k % ny
                ref, at = (refs[k], 0) if dz != 1 else (refs[-2], dy * 2 * rows)
                block = (z ^ turned(z, dz)) * ny + lax.rem(y + dy, ny)
                refs[-1][aligned(block, 2 * rows), :] = ref[at : at + 2 * rows, :]

        def near_body(own, sib, full, f_own, f_sib):
            for ref, out in ((own, f_own), (sib, f_sib)):
                features_of([ref[:, k * span : (k + 1) * span] for k in range(nz)], full, out)

        def far_body(*refs):
            features_of([ref[...] for ref in refs[:nz]], refs[nz], refs[nz + 1])

        def far_features(blocks):
            return run(
                "far_features", far_body, [((tokens, part), bf16)], [*blocks, w_full]
            )[0]

        def place_body(*refs):
            z, y, core, q = place()
            for j in range(4):
                refs[4][:, aligned(q ^ j, part)] = refs[j][...]

        w_order = [0, 3, 2, 1]
        others = range(1, ny)
        w_line = [None] * nz
        w_side = [None] * nz
        far_par, far_dia = [None] * nz, [None] * nz
        terms, moved_y = [None] * nz, [None] * nz

        def teacher_y(dz, *gates):
            w_side[dz] = [start(w_line[dz], along_y(-dy), *gates) for dy in others]

        def block_sum(dz, *parts, more=0):
            return add([terms[dz][0], *moved_y[dz], *parts], bf16, more)

        w_same, w_other = run(
            "cast_teacher",
            cast_body,
            [((rows, part), bf16), ((4 * rows + 2 * extra, part), bf16)],
            [teacher],
        )
        w_sib = start(w_other, sibling)
        first, near_own, c_own, second, third, mark = run(
            "cut_tokens",
            cut_body,
            [
                ((count, width), bf16)
                for count, width in (
                    (tokens, lead + span), (tokens, feat + part), (tokens, part),
                    (tokens + 2 * extra, span), (tokens, 2 * span), (tokens - extra, part),
                )
            ],
            [patches, cotangent],
        )
        message = start(first, partner)
        near_sib = start(near_own, sibling)
        (w_line[0],) = run(
            "join_teacher", join_body, [((2 * rows, part), bf16)], [w_same, w_sib]
        )
        w_line[3] = start(w_line[0], along_z(1))
        teacher_y(0)
        teacher_y(3, *w_side[0])
        (turn,) = run(
            "stack_teacher",
            stack_body,
            [((ny * 2 * rows + 2 * extra, part), bf16)],
            [after(w_line[0], near_sib), *w_side[0]],
        )
        turn = start(turn, along_z(-1))
        w_line[2] = start(w_line[3], along_z(1), turn)
        block = start(second, partner)
        c_other, c_par, far_par[0] = run(
            "split_message",
            split_body,
            [((tokens, part), bf16)] * 2 + [((tokens, span), bf16)],
            [after(message, near_sib)],
        )
        c_dia = start(c_other, sibling)
        far_dia[0] = start(far_par[0], sibling)
        wait(*w_side[3])
        gradient_block(0)
        both = start(third, partner)
        (far_par[1],) = run("take_block", first_body, [((tokens, span), bf16)], [block])
        far_dia[1] = start(far_par[1], sibling)
        wait(turn)
        gradient_block(1)
        onward = block_sum(3)
        teacher_y(2, onward)
        onward = start(onward, across_z(1))
        *pieces, far_par[2], far_par[3] = run(
            "take_blocks",
            take_body,
            [((tokens // 2, span), bf16)] * 2 + [((tokens, span), bf16)] * 2,
            [after(both, w_line[2])],
        )
        pieces = [start(piece, sibling) for piece in pieces]
        (far_dia[2],) = run("join_pieces", pieces_body, [((tokens, span), bf16)], pieces)
        gradient_block(2)
        onward = start(block_sum(2, onward), across_z(2))
        far_dia[3] = start(far_par[3], sibling, terms[1][0])
        (w_full,) = run(
            "fill_teacher",
            fill_body,
            [((feat, part), bf16)],
            [*(w for dz in w_order[:-1] for w in (w_line[dz], *w_side[dz])), turn],
        )
        f_par = start(far_features(far_par), partner)
        gradient_block(3)
        f_dia = start(far_features(far_dia), diagonal)
        back = start(block_sum(1), across_z(1))
        f_own, f_sib = run(
            "near_features",
            near_body,
            [((tokens, part), bf16)] * 2,
            [near_own, near_sib, w_full],
        )
        f_sib = start(f_sib, sibling)
        wait(f_par, f_dia)
        pieces = [terms[0][0], *moved_y[0], onward, back]
        spacer = start(mark, sibling, onward)
        if pair_groups > 1:
            total = add(pieces, f32)
            sent = total.astype(bf16)
            pieces = [total] + [start(sent, along_g(dg)) for dg in range(1, pair_groups)]
        mine, other = run("sum_gradient", sum_body, [((rows, part), bf16)] * 2, [*pieces, spacer])
        g_par, g_dia, g_sib = (
            start(mine, partner), start(other, diagonal), start(other, sibling)
        )
        def update_body(quarters):
            def body(*refs):
                z, y, core, q = place()
                student, first, second, teach = refs[len(quarters) :][:4]
                outs, held, sems = refs[-6:-2], refs[-2], refs[-1]
                corr_one = 1.0 - beta_one**STEP
                corr_two = 1.0 - beta_two**STEP
                copies = []
                for i, j in enumerate(quarters):
                    at = (slice(None), aligned(q ^ j, part))
                    gradient = refs[i][...].astype(f32)
                    new_first = beta_one * first[at] + (1.0 - beta_one) * gradient
                    new_second = beta_two * second[at] + (1.0 - beta_two) * gradient * gradient
                    direction = new_first / corr_one / (jnp.sqrt(new_second / corr_two) + adam_eps)
                    weights = student[at]
                    new_student = weights - learn_rate * (direction + decay_rate * weights)
                    new_teacher = ema_keep * teach[at] + (1.0 - ema_keep) * new_student
                    for k, new in enumerate((new_student, new_first, new_second, new_teacher)):
                        held[4 * i + k] = new
                        copies.append(
                            pltpu.make_async_copy(
                                held.at[4 * i + k], outs[k].at[at], sems.at[4 * i + k]
                            )
                        )
                        copies[-1].start()
                for copy in copies:
                    copy.wait()

            return body

        def update(name, quarters, grads, begun):
            inputs = [after(grads[0], *clock), *grads[1:]]
            inputs += [student, first_moment, second_moment, teacher]
            with jax.named_scope(name):
                out = pl.pallas_call(
                    update_body(quarters),
                    out_shape=[jax.ShapeDtypeStruct((rows, outw), f32)] * 4,
                    in_specs=[VMEM] * len(inputs) + [ANY] * len(begun),
                    out_specs=[ANY] * 4,
                    input_output_aliases={len(inputs) + k: k for k in range(len(begun))},
                    scratch_shapes=[
                        pltpu.VMEM((4 * len(quarters), rows, part), f32),
                        pltpu.SemaphoreType.DMA((4 * len(quarters),)),
                    ],
                    cost_estimate=pl.CostEstimate(flops=1, bytes_accessed=1, transcendentals=0),
                    compiler_params=pltpu.CompilerParams(vmem_limit_bytes=16 * 2**20),
                )(*inputs, *begun)
            clock[:] = out[:1]
            return out

        new = update("update_near", (0, 1), [mine, g_sib], [])
        (features,) = run(
            "place_features",
            place_body,
            [((tokens, outw), bf16)],
            [f_own, f_sib, f_par, f_dia],
        )
        new = update("update_partner", (2,), [g_par], new)
        new = update("update_diagonal", (3,), [g_dia], new)
        return (features, *new)

    tokens_placed, weights_placed = P(("fsdp", "rep"), None), P("fsdp", None)
    return jax.shard_map(
        per_device,
        mesh=mesh,
        in_specs=(tokens_placed,) * 2 + (weights_placed,) * 4,
        out_specs=(tokens_placed,) + (weights_placed,) * 4,
        check_vma=False,
    )
```

```python
import math

import jax
import jax.numpy as jnp
from jax import lax
from jax.experimental import pallas as pl
from jax.experimental.pallas import tpu as pltpu
from jax.sharding import PartitionSpec as P

STEP = 100

beta_one = 0.9
beta_two = 0.999
adam_eps = 1e-08
learn_rate = 0.1
decay_rate = 0.04
ema_keep = 0.994

bf16, f32 = jnp.bfloat16, jnp.float32
VMEM = pl.BlockSpec(memory_space=pltpu.VMEM)
ANY = pl.BlockSpec(memory_space=pl.ANY)


def call(name, body, outs, inputs, scratch=()):
    shapes = [jax.ShapeDtypeStruct(*out) for out in outs]
    moved = sum(a.size * a.dtype.itemsize for a in (*inputs, *shapes))
    held = sum(4 * math.prod(getattr(s, "shape", ())) for s in scratch)
    with jax.named_scope(name):
        return pl.pallas_call(
            body,
            out_shape=shapes,
            in_specs=[VMEM] * len(inputs),
            out_specs=[VMEM] * len(shapes),
            scratch_shapes=list(scratch),
            cost_estimate=pl.CostEstimate(flops=1, bytes_accessed=1, transcendentals=0),
            compiler_params=pltpu.CompilerParams(vmem_limit_bytes=moved + held + 4 * 2**20),
        )(*inputs)


def after(value, *others):
    return lax.optimization_barrier((value, *others))[0]


def aligned(index, size):
    return pl.ds(pl.multiple_of(index * size, size), size)


def solution(mesh):
    n, r = mesh.shape["fsdp"], mesh.shape["rep"]
    nz = 4
    ny = n // (2 * nz)
    pair_groups = r // 2

    def send(value, move):
        perm = []
        for f in range(n):
            for p in range(r):
                z, y, c = f // (2 * ny), f // 2 % ny, f % 2
                z, y, c, g, h = move(z, y, c, p // 2, p % 2)
                perm.append((f * r + p, ((z * ny + y) * 2 + c) * r + g * 2 + h))
        return lax.ppermute(value, ("fsdp", "rep"), perm)

    def sibling(z, y, c, g, h):
        return z, y, 1 - c, g, h

    def partner(z, y, c, g, h):
        return z, y, c, g, 1 - h

    def diagonal(z, y, c, g, h):
        return z, y, 1 - c, g, 1 - h

    def turned(z, d):
        p = ((z ^ (z >> 1)) + d) & 3
        return p ^ (p >> 1)

    def along_z(d):
        return lambda z, y, c, g, h: (turned(z, d), y, c, g, h)

    def across_z(d):
        return lambda z, y, c, g, h: (z ^ d, y, c, g, h)

    def along_y(d):
        return lambda z, y, c, g, h: (z, (y + d) % ny, c, g, h)

    def along_g(d):
        return lambda z, y, c, g, h: (z, y, c, (g + d) % pair_groups, h)

    def place():
        f = lax.axis_index("fsdp")
        core = lax.rem(f, 2)
        return f // (2 * ny), lax.rem(f // 2, ny), core, lax.rem(lax.axis_index("rep"), 2) * 2 + core

    def per_device(patches, cotangent, student, first_moment, second_moment, teacher):
        tokens, feat = patches.shape
        outw = cotangent.shape[1]
        rows = teacher.shape[0]
        part = outw // 4
        span = feat // nz
        g_order = [3, 2, 1, 0]
        lead = 2 * part
        extra = 16

        def cut_body(p, c, first, near, c_own, second, third, mark):
            z, y, core, q = place()
            mark[...] = c[: mark.shape[0], :part]
            first[:, :lead] = c[:, aligned(1 - q // 2, lead)]
            for k, dz in enumerate(g_order):
                block = p[:, aligned(z ^ dz, span)]
                near[:, k * span : (k + 1) * span] = block
                if k == 0:
                    first[:, lead:] = block
                elif k == 1:
                    second[:tokens, :] = block
                    second[tokens:, :] = block[: second.shape[0] - tokens, :]
                else:
                    third[:, (k - 2) * span : (k - 1) * span] = block
            near[:, feat:] = c[:, aligned(q ^ 1, part)]
            c_own[...] = c[:, aligned(q, part)]

        def split_body(message, c_sib, c_here, block):
            z, y, core, q = place()
            c_sib[...] = message[:, aligned(1 - core, part)]
            c_here[...] = message[:, aligned(core, part)]
            block[...] = message[:, lead:]

        def first_body(message, block):
            block[...] = message[:tokens, :]

        def take_body(message, upper, lower, first, second):
            first[...] = message[:, :span]
            second[...] = message[:, span:]
            upper[...] = message[: tokens // 2, :span]
            lower[...] = message[tokens // 2 :, :span]

        def pieces_body(upper, lower, block):
            block[: tokens // 2, :] = upper[...]
            block[tokens // 2 :, :] = lower[...]

        clock = []

        def run(name, body, outs, inputs, *scratch, **options):
            first = after(inputs[0], *clock) if clock else inputs[0]
            out = call(name, body, outs, [first, *inputs[1:]], *scratch, **options)
            clock[:] = out[:1]
            return out

        def start(value, move, *others):
            return send(after(value, *others) if others else value, move)

        def wait(*values):
            clock.extend(values)

        def cast_body(t, same, other):
            z, y, core, q = place()
            same[...] = t[:, aligned(q, part)].astype(bf16)
            other[:rows, :] = t[:, aligned(q ^ 1, part)].astype(bf16)
            other[rows:, :] = jnp.zeros((other.shape[0] - rows, part), bf16)

        def join_body(same, sib, out):
            z, y, core, q = place()
            out[aligned(core, rows), :] = same[...]
            out[aligned(1 - core, rows), :] = sib[:rows, :]

        def stack_body(*refs):
            for k, ref in enumerate(refs[:-1]):
                refs[-1][k * 2 * rows : (k + 1) * 2 * rows, :] = ref[...]
            refs[-1][ny * 2 * rows :, :] = refs[0][: 2 * extra, :]

        def terms_body(k):
            def body(own, sib, par, dia, c0, c_par, c_dia, *outs):
                z, y, core, q = place()
                whole = outs[-1]
                near = slice(k * span, (k + 1) * span)
                total = None
                for p, c in (
                    (own[:, near], c0[...]),
                    (sib[:, near], sib[:, feat:]),
                    (par[...], c_par[...]),
                    (dia[...], c_dia[...]),
                ):
                    term = lax.dot_general(
                        p, c, (((0,), (0,)), ((), ())), preferred_element_type=f32
                    )
                    total = term if total is None else total + term
                whole[...] = total
                for dy in range(ny):
                    block = whole[aligned(lax.rem(y + dy, ny), 2 * rows), :]
                    outs[dy][: 2 * rows, :] = block.astype(outs[dy].dtype)
                    if outs[dy].shape[0] > 2 * rows:
                        rest = (outs[dy].shape[0] - 2 * rows, part)
                        outs[dy][2 * rows :, :] = jnp.zeros(rest, outs[dy].dtype)

            return body

        def gradient_block(k):
            dz = g_order[k]
            terms[dz] = run(
                "gradient_block",
                terms_body(k),
                [((2 * rows, part), f32)]
                + [((2 * rows + (2 * extra, extra, 0, 0)[k], part), bf16)] * (ny - 1),
                [near_own, near_sib, far_par[k], far_dia[k], c_own, c_par, c_dia],
                scratch=[pltpu.VMEM((span, part), f32)],
            )
            moved_y[dz] = [start(terms[dz][dy], along_y(dy)) for dy in others]

        def add_body(*refs):
            total = sum(ref[: 2 * rows, :].astype(f32) for ref in refs[:-1])
            refs[-1][: 2 * rows, :] = total.astype(refs[-1].dtype)
            if refs[-1].shape[0] > 2 * rows:
                rest = (refs[-1].shape[0] - 2 * rows, part)
                refs[-1][2 * rows :, :] = jnp.zeros(rest, refs[-1].dtype)

        def add(values, dtype, more=0):
            return run("add_blocks", add_body, [((2 * rows + more, part), dtype)], values)[0]

        def sum_body(*refs):
            z, y, core, q = place()
            for out, at in zip(refs[-2:], (aligned(core, rows), aligned(1 - core, rows))):
                out[...] = sum(ref[at, :].astype(f32) for ref in refs[:-3]).astype(bf16)

        def features_of(blocks, full, out):
            total = sum(
                jnp.dot(
                    block, full[dz * span : (dz + 1) * span, :], preferred_element_type=f32
                )
                for block, dz in zip(blocks, g_order)
            )
            out[...] = (total * feat ** (-0.5)).astype(bf16)

        def fill_body(*refs):
            z, y, core, q = place()
            for k in range(nz * ny):
                dz, dy = w_order[k // ny], k % ny
                ref, at = (refs[k], 0) if dz != 1 else (refs[-2], dy * 2 * rows)
                block = (z ^ turned(z, dz)) * ny + lax.rem(y + dy, ny)
                refs[-1][aligned(block, 2 * rows), :] = ref[at : at + 2 * rows, :]

        def near_body(own, sib, full, f_own, f_sib):
            for ref, out in ((own, f_own), (sib, f_sib)):
                features_of([ref[:, k * span : (k + 1) * span] for k in range(nz)], full, out)

        def far_body(*refs):
            features_of([ref[...] for ref in refs[:nz]], refs[nz], refs[nz + 1])

        def far_features(blocks):
            return run(
                "far_features", far_body, [((tokens, part), bf16)], [*blocks, w_full]
            )[0]

        def place_body(*refs):
            z, y, core, q = place()
            for j in range(4):
                refs[4][:, aligned(q ^ j, part)] = refs[j][...]

        w_order = [0, 3, 2, 1]
        others = range(1, ny)
        w_line = [None] * nz
        w_side = [None] * nz
        far_par, far_dia = [None] * nz, [None] * nz
        terms, moved_y = [None] * nz, [None] * nz

        def teacher_y(dz, *gates):
            w_side[dz] = [start(w_line[dz], along_y(-dy), *gates) for dy in others]

        def block_sum(dz, *parts, more=0):
            return add([terms[dz][0], *moved_y[dz], *parts], bf16, more)

        first, near_own, c_own, second, third, mark = run(
            "cut_tokens",
            cut_body,
            [
                ((count, width), bf16)
                for count, width in (
                    (tokens, lead + span), (tokens, feat + part), (tokens, part),
                    (tokens + 2 * extra, span), (tokens, 2 * span), (tokens - extra, part),
                )
            ],
            [patches, cotangent],
        )
        w_same, w_other = run(
            "cast_teacher",
            cast_body,
            [((rows, part), bf16), ((4 * rows + 2 * extra, part), bf16)],
            [after(teacher, first)],
        )
        w_sib = start(w_other, sibling)
        message = start(first, partner)
        near_sib = start(near_own, sibling)
        (w_line[0],) = run(
            "join_teacher", join_body, [((2 * rows, part), bf16)], [w_same, w_sib]
        )
        w_line[3] = start(w_line[0], along_z(1))
        teacher_y(0)
        teacher_y(3, *w_side[0])
        (turn,) = run(
            "stack_teacher",
            stack_body,
            [((ny * 2 * rows + 2 * extra, part), bf16)],
            [after(w_line[0], near_sib), *w_side[0]],
        )
        w_line[2] = start(w_line[3], along_z(1))
        turn = start(turn, along_z(-1), w_line[2])
        block = start(second, partner)
        c_other, c_par, far_par[0] = run(
            "split_message",
            split_body,
            [((tokens, part), bf16)] * 2 + [((tokens, span), bf16)],
            [after(message, near_sib)],
        )
        c_dia = start(c_other, sibling)
        far_dia[0] = start(far_par[0], sibling)
        wait(*w_side[3])
        gradient_block(0)
        both = start(third, partner)
        (far_par[1],) = run("take_block", first_body, [((tokens, span), bf16)], [block])
        far_dia[1] = start(far_par[1], sibling)
        gradient_block(1)
        onward = block_sum(3)
        teacher_y(2, onward)
        onward = start(onward, across_z(1))
        *pieces, far_par[2], far_par[3] = run(
            "take_blocks",
            take_body,
            [((tokens // 2, span), bf16)] * 2 + [((tokens, span), bf16)] * 2,
            [after(both, turn)],
        )
        pieces = [start(piece, sibling) for piece in pieces]
        (far_dia[2],) = run("join_pieces", pieces_body, [((tokens, span), bf16)], pieces)
        gradient_block(2)
        onward = start(block_sum(2, onward), across_z(2))
        far_dia[3] = start(far_par[3], sibling, terms[1][0])
        (w_full,) = run(
            "fill_teacher",
            fill_body,
            [((feat, part), bf16)],
            [*(w for dz in w_order[:-1] for w in (w_line[dz], *w_side[dz])), turn],
        )
        f_par = start(far_features(far_par), partner)
        gradient_block(3)
        f_dia = start(far_features(far_dia), diagonal)
        back = start(block_sum(1), across_z(1))
        f_own, f_sib = run(
            "near_features",
            near_body,
            [((tokens, part), bf16)] * 2,
            [near_own, near_sib, w_full],
        )
        f_sib = start(f_sib, sibling)
        wait(f_par, f_dia)
        pieces = [terms[0][0], *moved_y[0], onward, back]
        spacer = start(mark, sibling, onward)
        if pair_groups > 1:
            total = add(pieces, f32)
            sent = total.astype(bf16)
            pieces = [total] + [start(sent, along_g(dg)) for dg in range(1, pair_groups)]
        mine, other = run("sum_gradient", sum_body, [((rows, part), bf16)] * 2, [*pieces, spacer])
        g_par, g_dia, g_sib = (
            start(mine, partner), start(other, diagonal), start(other, sibling)
        )
        def update_body(quarters):
            def body(*refs):
                z, y, core, q = place()
                student, first, second, teach = refs[len(quarters) :][:4]
                outs, held, sems = refs[-6:-2], refs[-2], refs[-1]
                corr_one = 1.0 - beta_one**STEP
                corr_two = 1.0 - beta_two**STEP
                copies = []
                for i, j in enumerate(quarters):
                    at = (slice(None), aligned(q ^ j, part))
                    gradient = refs[i][...].astype(f32)
                    new_first = beta_one * first[at] + (1.0 - beta_one) * gradient
                    new_second = beta_two * second[at] + (1.0 - beta_two) * gradient * gradient
                    direction = new_first / corr_one / (jnp.sqrt(new_second / corr_two) + adam_eps)
                    weights = student[at]
                    new_student = weights - learn_rate * (direction + decay_rate * weights)
                    new_teacher = ema_keep * teach[at] + (1.0 - ema_keep) * new_student
                    for k, new in enumerate((new_student, new_first, new_second, new_teacher)):
                        held[4 * i + k] = new
                        copies.append(
                            pltpu.make_async_copy(
                                held.at[4 * i + k], outs[k].at[at], sems.at[4 * i + k]
                            )
                        )
                        copies[-1].start()
                for copy in copies:
                    copy.wait()

            return body

        def update(name, quarters, grads, begun):
            inputs = [after(grads[0], *clock), *grads[1:]]
            inputs += [student, first_moment, second_moment, teacher]
            with jax.named_scope(name):
                out = pl.pallas_call(
                    update_body(quarters),
                    out_shape=[jax.ShapeDtypeStruct((rows, outw), f32)] * 4,
                    in_specs=[VMEM] * len(inputs) + [ANY] * len(begun),
                    out_specs=[ANY] * 4,
                    input_output_aliases={len(inputs) + k: k for k in range(len(begun))},
                    scratch_shapes=[
                        pltpu.VMEM((4 * len(quarters), rows, part), f32),
                        pltpu.SemaphoreType.DMA((4 * len(quarters),)),
                    ],
                    cost_estimate=pl.CostEstimate(flops=1, bytes_accessed=1, transcendentals=0),
                    compiler_params=pltpu.CompilerParams(vmem_limit_bytes=16 * 2**20),
                )(*inputs, *begun)
            clock[:] = out[:1]
            return out

        new = update("update_near", (0, 1), [mine, g_sib], [])
        (features,) = run(
            "place_features",
            place_body,
            [((tokens, outw), bf16)],
            [f_own, f_sib, f_par, f_dia],
        )
        new = update("update_partner", (2,), [g_par], new)
        new = update("update_diagonal", (3,), [g_dia], new)
        return (features, *new)

    tokens_placed, weights_placed = P(("fsdp", "rep"), None), P("fsdp", None)
    return jax.shard_map(
        per_device,
        mesh=mesh,
        in_specs=(tokens_placed,) * 2 + (weights_placed,) * 4,
        out_specs=(tokens_placed,) + (weights_placed,) * 4,
        check_vma=False,
    )
```

```python
import math

import jax
import jax.numpy as jnp
from jax import lax
from jax.experimental import pallas as pl
from jax.experimental.pallas import tpu as pltpu
from jax.sharding import PartitionSpec as P

STEP = 100

beta_one = 0.9
beta_two = 0.999
adam_eps = 1e-08
learn_rate = 0.1
decay_rate = 0.04
ema_keep = 0.994

bf16, f32 = jnp.bfloat16, jnp.float32
VMEM = pl.BlockSpec(memory_space=pltpu.VMEM)
ANY = pl.BlockSpec(memory_space=pl.ANY)


def call(name, body, outs, inputs, scratch=()):
    shapes = [jax.ShapeDtypeStruct(*out) for out in outs]
    moved = sum(a.size * a.dtype.itemsize for a in (*inputs, *shapes))
    held = sum(4 * math.prod(getattr(s, "shape", ())) for s in scratch)
    with jax.named_scope(name):
        return pl.pallas_call(
            body,
            out_shape=shapes,
            in_specs=[VMEM] * len(inputs),
            out_specs=[VMEM] * len(shapes),
            scratch_shapes=list(scratch),
            cost_estimate=pl.CostEstimate(flops=1, bytes_accessed=1, transcendentals=0),
            compiler_params=pltpu.CompilerParams(vmem_limit_bytes=moved + held + 4 * 2**20),
        )(*inputs)


def after(value, *others):
    return lax.optimization_barrier((value, *others))[0]


def aligned(index, size):
    return pl.ds(pl.multiple_of(index * size, size), size)


def solution(mesh):
    n, r = mesh.shape["fsdp"], mesh.shape["rep"]
    nz = 4
    ny = n // (2 * nz)
    pair_groups = r // 2

    def send(value, move):
        perm = []
        for f in range(n):
            for p in range(r):
                z, y, c = f // (2 * ny), f // 2 % ny, f % 2
                z, y, c, g, h = move(z, y, c, p // 2, p % 2)
                perm.append((f * r + p, ((z * ny + y) * 2 + c) * r + g * 2 + h))
        return lax.ppermute(value, ("fsdp", "rep"), perm)

    def sibling(z, y, c, g, h):
        return z, y, 1 - c, g, h

    def partner(z, y, c, g, h):
        return z, y, c, g, 1 - h

    def diagonal(z, y, c, g, h):
        return z, y, 1 - c, g, 1 - h

    def turned(z, d):
        p = ((z ^ (z >> 1)) + d) & 3
        return p ^ (p >> 1)

    def along_z(d):
        return lambda z, y, c, g, h: (turned(z, d), y, c, g, h)

    def across_z(d):
        return lambda z, y, c, g, h: (z ^ d, y, c, g, h)

    def along_y(d):
        return lambda z, y, c, g, h: (z, (y + d) % ny, c, g, h)

    def along_g(d):
        return lambda z, y, c, g, h: (z, y, c, (g + d) % pair_groups, h)

    def place():
        f = lax.axis_index("fsdp")
        core = lax.rem(f, 2)
        return f // (2 * ny), lax.rem(f // 2, ny), core, lax.rem(lax.axis_index("rep"), 2) * 2 + core

    def per_device(patches, cotangent, student, first_moment, second_moment, teacher):
        tokens, feat = patches.shape
        outw = cotangent.shape[1]
        rows = teacher.shape[0]
        part = outw // 4
        span = feat // nz
        g_order = [3, 2, 1, 0]
        lead = 2 * part
        extra = 16

        def cut_body(p, c, first, near, c_own, second, third, mark):
            z, y, core, q = place()
            mark[...] = c[: mark.shape[0], :part]
            first[:, :lead] = c[:, aligned(1 - q // 2, lead)]
            for k, dz in enumerate(g_order):
                block = p[:, aligned(z ^ dz, span)]
                near[:, k * span : (k + 1) * span] = block
                if k == 0:
                    first[:, lead:] = block
                elif k == 1:
                    second[:tokens, :] = block
                    second[tokens:, :] = block[: second.shape[0] - tokens, :]
                else:
                    third[:, (k - 2) * span : (k - 1) * span] = block
            near[:, feat:] = c[:, aligned(q ^ 1, part)]
            c_own[...] = c[:, aligned(q, part)]

        def split_body(message, c_sib, c_here, block):
            z, y, core, q = place()
            c_sib[...] = message[:, aligned(1 - core, part)]
            c_here[...] = message[:, aligned(core, part)]
            block[...] = message[:, lead:]

        def first_body(message, block):
            block[...] = message[:tokens, :]

        def take_body(message, upper, lower, first, second):
            first[...] = message[:, :span]
            second[...] = message[:, span:]
            upper[...] = message[: tokens // 2, :span]
            lower[...] = message[tokens // 2 :, :span]

        def pieces_body(upper, lower, block):
            block[: tokens // 2, :] = upper[...]
            block[tokens // 2 :, :] = lower[...]

        clock = []

        def run(name, body, outs, inputs, *scratch, **options):
            first = after(inputs[0], *clock) if clock else inputs[0]
            out = call(name, body, outs, [first, *inputs[1:]], *scratch, **options)
            clock[:] = out[:1]
            return out

        def start(value, move, *others):
            return send(after(value, *others) if others else value, move)

        def wait(*values):
            clock.extend(values)

        def cast_body(t, same, other):
            z, y, core, q = place()
            same[...] = t[:, aligned(q, part)].astype(bf16)
            other[:rows, :] = t[:, aligned(q ^ 1, part)].astype(bf16)
            other[rows:, :] = jnp.zeros((other.shape[0] - rows, part), bf16)

        def join_body(same, sib, out):
            z, y, core, q = place()
            out[aligned(core, rows), :] = same[...]
            out[aligned(1 - core, rows), :] = sib[:rows, :]

        def stack_body(*refs):
            for k, ref in enumerate(refs[:-1]):
                refs[-1][k * 2 * rows : (k + 1) * 2 * rows, :] = ref[...]
            refs[-1][ny * 2 * rows :, :] = refs[0][: 2 * extra, :]

        def terms_body(k):
            def body(own, sib, par, dia, c0, c_par, c_dia, *outs):
                z, y, core, q = place()
                whole = outs[-1]
                near = slice(k * span, (k + 1) * span)
                total = None
                for p, c in (
                    (own[:, near], c0[...]),
                    (sib[:, near], sib[:, feat:]),
                    (par[...], c_par[...]),
                    (dia[...], c_dia[...]),
                ):
                    term = lax.dot_general(
                        p, c, (((0,), (0,)), ((), ())), preferred_element_type=f32
                    )
                    total = term if total is None else total + term
                whole[...] = total
                for dy in range(ny):
                    block = whole[aligned(lax.rem(y + dy, ny), 2 * rows), :]
                    outs[dy][: 2 * rows, :] = block.astype(outs[dy].dtype)
                    if outs[dy].shape[0] > 2 * rows:
                        rest = (outs[dy].shape[0] - 2 * rows, part)
                        outs[dy][2 * rows :, :] = jnp.zeros(rest, outs[dy].dtype)

            return body

        def block_y(dz, *gates):
            moved_y[dz] = [start(terms[dz][dy], along_y(dy), *gates) for dy in others]

        def gradient_block(k):
            dz = g_order[k]
            terms[dz] = run(
                "gradient_block",
                terms_body(k),
                [((2 * rows, part), f32)]
                + [((2 * rows + extra * (k == 0), part), bf16)] * (ny - 1),
                [near_own, near_sib, far_par[k], far_dia[k], c_own, c_par, c_dia],
                scratch=[pltpu.VMEM((span, part), f32)],
            )

        def add_body(*refs):
            total = sum(ref[: 2 * rows, :].astype(f32) for ref in refs[:-1])
            refs[-1][: 2 * rows, :] = total.astype(refs[-1].dtype)
            if refs[-1].shape[0] > 2 * rows:
                rest = (refs[-1].shape[0] - 2 * rows, part)
                refs[-1][2 * rows :, :] = jnp.zeros(rest, refs[-1].dtype)

        def add(values, dtype, more=0):
            return run("add_blocks", add_body, [((2 * rows + more, part), dtype)], values)[0]

        def sum_body(*refs):
            z, y, core, q = place()
            for out, at in zip(refs[-2:], (aligned(core, rows), aligned(1 - core, rows))):
                out[...] = sum(ref[at, :].astype(f32) for ref in refs[:-3]).astype(bf16)

        def features_of(blocks, full, out):
            total = sum(
                jnp.dot(
                    block, full[dz * span : (dz + 1) * span, :], preferred_element_type=f32
                )
                for block, dz in zip(blocks, g_order)
            )
            out[...] = (total * feat ** (-0.5)).astype(bf16)

        def fill_body(*refs):
            z, y, core, q = place()
            for k in range(nz * ny):
                dz, dy = w_order[k // ny], k % ny
                ref, at = (refs[k], 0) if dz != 1 else (refs[-2], dy * 2 * rows)
                block = (z ^ turned(z, dz)) * ny + lax.rem(y + dy, ny)
                refs[-1][aligned(block, 2 * rows), :] = ref[at : at + 2 * rows, :]

        def near_body(own, sib, full, f_own, f_sib):
            for ref, out in ((own, f_own), (sib, f_sib)):
                features_of([ref[:, k * span : (k + 1) * span] for k in range(nz)], full, out)

        def far_body(*refs):
            features_of([ref[...] for ref in refs[:nz]], refs[nz], refs[nz + 1])

        def far_features(blocks):
            return run(
                "far_features", far_body, [((tokens, part), bf16)], [*blocks, w_full]
            )[0]

        def place_body(*refs):
            z, y, core, q = place()
            for j in range(4):
                refs[4][:, aligned(q ^ j, part)] = refs[j][...]

        w_order = [0, 3, 2, 1]
        others = range(1, ny)
        w_line = [None] * nz
        w_side = [None] * nz
        far_par, far_dia = [None] * nz, [None] * nz
        terms, moved_y = [None] * nz, [None] * nz

        def teacher_y(dz, *gates):
            w_side[dz] = [start(w_line[dz], along_y(-dy), *gates) for dy in others]

        def block_sum(dz, *parts, more=0):
            return add([terms[dz][0], *moved_y[dz], *parts], bf16, more)

        first, near_own, c_own, second, third, mark = run(
            "cut_tokens",
            cut_body,
            [
                ((count, width), bf16)
                for count, width in (
                    (tokens, lead + span), (tokens, feat + part), (tokens, part),
                    (tokens + 2 * extra, span), (tokens, 2 * span), (tokens - extra, part),
                )
            ],
            [patches, cotangent],
        )
        w_same, w_other = run(
            "cast_teacher",
            cast_body,
            [((rows, part), bf16), ((4 * rows + 2 * extra, part), bf16)],
            [after(teacher, first)],
        )
        w_sib = start(w_other, sibling)
        message = start(first, partner)
        near_sib = start(near_own, sibling)
        (w_line[0],) = run(
            "join_teacher", join_body, [((2 * rows, part), bf16)], [w_same, w_sib]
        )
        w_line[3] = start(w_line[0], along_z(1))
        teacher_y(0)
        teacher_y(3, *w_side[0])
        (turn,) = run(
            "stack_teacher",
            stack_body,
            [((ny * 2 * rows + 2 * extra, part), bf16)],
            [after(w_line[0], near_sib), *w_side[0]],
        )
        w_line[2] = start(w_line[3], along_z(1))
        turn = start(turn, along_z(-1), w_line[2])
        block = start(second, partner)
        c_other, c_par, far_par[0] = run(
            "split_message",
            split_body,
            [((tokens, part), bf16)] * 2 + [((tokens, span), bf16)],
            [after(message, near_sib)],
        )
        c_dia = start(c_other, sibling)
        far_dia[0] = start(far_par[0], sibling)
        wait(*w_side[3])
        gradient_block(0)
        block_y(3)
        both = start(third, partner)
        (far_par[1],) = run("take_block", first_body, [((tokens, span), bf16)], [block])
        far_dia[1] = start(far_par[1], sibling)
        gradient_block(1)
        onward = block_sum(3)
        block_y(2, onward)
        teacher_y(2, onward)
        onward = start(onward, across_z(1))
        *pieces, far_par[2], far_par[3] = run(
            "take_blocks",
            take_body,
            [((tokens // 2, span), bf16)] * 2 + [((tokens, span), bf16)] * 2,
            [after(both, turn)],
        )
        pieces = [start(piece, sibling) for piece in pieces]
        (far_dia[2],) = run("join_pieces", pieces_body, [((tokens, span), bf16)], pieces)
        gradient_block(2)
        block_y(1)
        onward = start(block_sum(2, onward), across_z(2))
        far_dia[3] = start(far_par[3], sibling, terms[1][0])
        (w_full,) = run(
            "fill_teacher",
            fill_body,
            [((feat, part), bf16)],
            [*(w for dz in w_order[:-1] for w in (w_line[dz], *w_side[dz])), turn],
        )
        f_par = start(far_features(far_par), partner)
        gradient_block(3)
        block_y(0)
        f_dia = start(far_features(far_dia), diagonal)
        back = start(block_sum(1), across_z(1))
        f_own, f_sib = run(
            "near_features",
            near_body,
            [((tokens, part), bf16)] * 2,
            [near_own, near_sib, w_full],
        )
        f_sib = start(f_sib, sibling)
        wait(f_par, f_dia)
        pieces = [terms[0][0], *moved_y[0], onward, back]
        spacer = start(mark, sibling, onward)
        if pair_groups > 1:
            total = add(pieces, f32)
            sent = total.astype(bf16)
            pieces = [total] + [start(sent, along_g(dg)) for dg in range(1, pair_groups)]
        mine, other = run("sum_gradient", sum_body, [((rows, part), bf16)] * 2, [*pieces, spacer])
        g_par, g_dia, g_sib = (
            start(mine, partner), start(other, diagonal), start(other, sibling)
        )
        def update_body(quarters):
            def body(*refs):
                z, y, core, q = place()
                student, first, second, teach = refs[len(quarters) :][:4]
                outs, held, sems = refs[-6:-2], refs[-2], refs[-1]
                corr_one = 1.0 - beta_one**STEP
                corr_two = 1.0 - beta_two**STEP
                copies = []
                for i, j in enumerate(quarters):
                    at = (slice(None), aligned(q ^ j, part))
                    gradient = refs[i][...].astype(f32)
                    new_first = beta_one * first[at] + (1.0 - beta_one) * gradient
                    new_second = beta_two * second[at] + (1.0 - beta_two) * gradient * gradient
                    direction = new_first / corr_one / (jnp.sqrt(new_second / corr_two) + adam_eps)
                    weights = student[at]
                    new_student = weights - learn_rate * (direction + decay_rate * weights)
                    new_teacher = ema_keep * teach[at] + (1.0 - ema_keep) * new_student
                    for k, new in enumerate((new_student, new_first, new_second, new_teacher)):
                        held[4 * i + k] = new
                        copies.append(
                            pltpu.make_async_copy(
                                held.at[4 * i + k], outs[k].at[at], sems.at[4 * i + k]
                            )
                        )
                        copies[-1].start()
                for copy in copies:
                    copy.wait()

            return body

        def update(name, quarters, grads, begun):
            inputs = [after(grads[0], *clock), *grads[1:]]
            inputs += [student, first_moment, second_moment, teacher]
            with jax.named_scope(name):
                out = pl.pallas_call(
                    update_body(quarters),
                    out_shape=[jax.ShapeDtypeStruct((rows, outw), f32)] * 4,
                    in_specs=[VMEM] * len(inputs) + [ANY] * len(begun),
                    out_specs=[ANY] * 4,
                    input_output_aliases={len(inputs) + k: k for k in range(len(begun))},
                    scratch_shapes=[
                        pltpu.VMEM((4 * len(quarters), rows, part), f32),
                        pltpu.SemaphoreType.DMA((4 * len(quarters),)),
                    ],
                    cost_estimate=pl.CostEstimate(flops=1, bytes_accessed=1, transcendentals=0),
                    compiler_params=pltpu.CompilerParams(vmem_limit_bytes=16 * 2**20),
                )(*inputs, *begun)
            clock[:] = out[:1]
            return out

        new = update("update_near", (0, 1), [mine, g_sib], [])
        (features,) = run(
            "place_features",
            place_body,
            [((tokens, outw), bf16)],
            [f_own, f_sib, f_par, f_dia],
        )
        new = update("update_partner", (2,), [g_par], new)
        new = update("update_diagonal", (3,), [g_dia], new)
        return (features, *new)

    tokens_placed, weights_placed = P(("fsdp", "rep"), None), P("fsdp", None)
    return jax.shard_map(
        per_device,
        mesh=mesh,
        in_specs=(tokens_placed,) * 2 + (weights_placed,) * 4,
        out_specs=(tokens_placed,) + (weights_placed,) * 4,
        check_vma=False,
    )
```

```python
import math

import jax
import jax.numpy as jnp
from jax import lax
from jax.experimental import pallas as pl
from jax.experimental.pallas import tpu as pltpu
from jax.sharding import PartitionSpec as P

STEP = 100

beta_one = 0.9
beta_two = 0.999
adam_eps = 1e-08
learn_rate = 0.1
decay_rate = 0.04
ema_keep = 0.994

bf16, f32 = jnp.bfloat16, jnp.float32
VMEM = pl.BlockSpec(memory_space=pltpu.VMEM)
ANY = pl.BlockSpec(memory_space=pl.ANY)


def call(name, body, outs, inputs, scratch=()):
    shapes = [jax.ShapeDtypeStruct(*out) for out in outs]
    moved = sum(a.size * a.dtype.itemsize for a in (*inputs, *shapes))
    held = sum(4 * math.prod(getattr(s, "shape", ())) for s in scratch)
    with jax.named_scope(name):
        return pl.pallas_call(
            body,
            out_shape=shapes,
            in_specs=[VMEM] * len(inputs),
            out_specs=[VMEM] * len(shapes),
            scratch_shapes=list(scratch),
            cost_estimate=pl.CostEstimate(flops=1, bytes_accessed=1, transcendentals=0),
            compiler_params=pltpu.CompilerParams(vmem_limit_bytes=moved + held + 4 * 2**20),
        )(*inputs)


def after(value, *others):
    return lax.optimization_barrier((value, *others))[0]


def aligned(index, size):
    return pl.ds(pl.multiple_of(index * size, size), size)


def solution(mesh):
    n, r = mesh.shape["fsdp"], mesh.shape["rep"]
    nz = 4
    ny = n // (2 * nz)
    pair_groups = r // 2

    def send(value, move):
        perm = []
        for f in range(n):
            for p in range(r):
                z, y, c = f // (2 * ny), f // 2 % ny, f % 2
                z, y, c, g, h = move(z, y, c, p // 2, p % 2)
                perm.append((f * r + p, ((z * ny + y) * 2 + c) * r + g * 2 + h))
        return lax.ppermute(value, ("fsdp", "rep"), perm)

    def sibling(z, y, c, g, h):
        return z, y, 1 - c, g, h

    def partner(z, y, c, g, h):
        return z, y, c, g, 1 - h

    def diagonal(z, y, c, g, h):
        return z, y, 1 - c, g, 1 - h

    def turned(z, d):
        p = ((z ^ (z >> 1)) + d) & 3
        return p ^ (p >> 1)

    def along_z(d):
        return lambda z, y, c, g, h: (turned(z, d), y, c, g, h)

    def across_z(d):
        return lambda z, y, c, g, h: (z ^ d, y, c, g, h)

    def along_y(d):
        return lambda z, y, c, g, h: (z, (y + d) % ny, c, g, h)

    def along_g(d):
        return lambda z, y, c, g, h: (z, y, c, (g + d) % pair_groups, h)

    def place():
        f = lax.axis_index("fsdp")
        core = lax.rem(f, 2)
        return f // (2 * ny), lax.rem(f // 2, ny), core, lax.rem(lax.axis_index("rep"), 2) * 2 + core

    def per_device(patches, cotangent, student, first_moment, second_moment, teacher):
        tokens, feat = patches.shape
        outw = cotangent.shape[1]
        rows = teacher.shape[0]
        part = outw // 4
        span = feat // nz
        g_order = [3, 2, 1, 0]
        lead = 2 * part
        extra = 16

        def cut_body(p, c, first, near, c_own, second, third, mark):
            z, y, core, q = place()
            mark[...] = c[: mark.shape[0], :part]
            first[:, :lead] = c[:, aligned(1 - q // 2, lead)]
            for k, dz in enumerate(g_order):
                block = p[:, aligned(z ^ dz, span)]
                near[:, k * span : (k + 1) * span] = block
                if k == 0:
                    first[:, lead:] = block
                elif k == 1:
                    second[:tokens, :] = block
                    second[tokens:, :] = block[: second.shape[0] - tokens, :]
                else:
                    third[:, (k - 2) * span : (k - 1) * span] = block
            near[:, feat:] = c[:, aligned(q ^ 1, part)]
            c_own[...] = c[:, aligned(q, part)]

        def split_body(message, c_sib, c_here, block):
            z, y, core, q = place()
            c_sib[...] = message[:, aligned(1 - core, part)]
            c_here[...] = message[:, aligned(core, part)]
            block[...] = message[:, lead:]

        def first_body(message, block):
            block[...] = message[:tokens, :]

        def take_body(message, upper, lower, first, second):
            first[...] = message[:, :span]
            second[...] = message[:, span:]
            upper[...] = message[: tokens // 2, :span]
            lower[...] = message[tokens // 2 :, :span]

        def pieces_body(upper, lower, block):
            block[: tokens // 2, :] = upper[...]
            block[tokens // 2 :, :] = lower[...]

        clock = []

        def run(name, body, outs, inputs, *scratch, **options):
            first = after(inputs[0], *clock) if clock else inputs[0]
            out = call(name, body, outs, [first, *inputs[1:]], *scratch, **options)
            clock[:] = out[:1]
            return out

        def start(value, move, *others):
            return send(after(value, *others) if others else value, move)

        def wait(*values):
            clock.extend(values)

        def cast_body(t, same, other):
            z, y, core, q = place()
            same[...] = t[:, aligned(q, part)].astype(bf16)
            other[:rows, :] = t[:, aligned(q ^ 1, part)].astype(bf16)
            other[rows:, :] = jnp.zeros((other.shape[0] - rows, part), bf16)

        def join_body(same, sib, out):
            z, y, core, q = place()
            out[aligned(core, rows), :] = same[...]
            out[aligned(1 - core, rows), :] = sib[:rows, :]

        def stack_body(*refs):
            for k, ref in enumerate(refs[:-1]):
                refs[-1][k * 2 * rows : (k + 1) * 2 * rows, :] = ref[...]
            refs[-1][ny * 2 * rows :, :] = refs[0][: 2 * extra, :]

        def terms_body(k):
            def body(own, sib, par, dia, c0, c_par, c_dia, *outs):
                z, y, core, q = place()
                whole = outs[-1]
                near = slice(k * span, (k + 1) * span)
                total = None
                for p, c in (
                    (own[:, near], c0[...]),
                    (sib[:, near], sib[:, feat:]),
                    (par[...], c_par[...]),
                    (dia[...], c_dia[...]),
                ):
                    term = lax.dot_general(
                        p, c, (((0,), (0,)), ((), ())), preferred_element_type=f32
                    )
                    total = term if total is None else total + term
                whole[...] = total
                for dy in range(ny):
                    block = whole[aligned(lax.rem(y + dy, ny), 2 * rows), :]
                    outs[dy][: 2 * rows, :] = block.astype(outs[dy].dtype)
                    if outs[dy].shape[0] > 2 * rows:
                        rest = (outs[dy].shape[0] - 2 * rows, part)
                        outs[dy][2 * rows :, :] = jnp.zeros(rest, outs[dy].dtype)

            return body

        def block_y(dz, *gates):
            moved_y[dz] = [start(terms[dz][dy], along_y(dy), *gates) for dy in others]

        def gradient_block(k):
            dz = g_order[k]
            terms[dz] = run(
                "gradient_block",
                terms_body(k),
                [((2 * rows, part), f32)]
                + [((2 * rows + extra * (k < 2), part), bf16)] * (ny - 1),
                [near_own, near_sib, far_par[k], far_dia[k], c_own, c_par, c_dia],
                scratch=[pltpu.VMEM((span, part), f32)],
            )

        def add_body(*refs):
            total = sum(ref[: 2 * rows, :].astype(f32) for ref in refs[:-1])
            refs[-1][: 2 * rows, :] = total.astype(refs[-1].dtype)
            if refs[-1].shape[0] > 2 * rows:
                rest = (refs[-1].shape[0] - 2 * rows, part)
                refs[-1][2 * rows :, :] = jnp.zeros(rest, refs[-1].dtype)

        def add(values, dtype, more=0):
            return run("add_blocks", add_body, [((2 * rows + more, part), dtype)], values)[0]

        def halves_sum_body(*refs):
            z, y, core, q = place()
            for out, owner in zip(refs[-2:], (1 - core, core)):
                at = aligned(owner, rows)
                out[...] = sum(ref[at, :].astype(f32) for ref in refs[:-2]).astype(bf16)

        def rows_sum_body(mine, count):
            def body(*refs):
                z, y, core, q = place()
                at = aligned(core if mine else 1 - core, rows)
                total = sum(ref[at, :].astype(f32) for ref in refs[:count])
                total = (total + refs[count][...].astype(f32)).astype(refs[-1].dtype)
                refs[-1][:rows, :] = total
                if refs[-1].shape[0] > rows:
                    refs[-1][rows:, :] = total[: refs[-1].shape[0] - rows, :]

            return body

        def add_rows_body(*refs):
            refs[-1][...] = sum(ref[...].astype(f32) for ref in refs[:-1]).astype(bf16)

        def gradient_rows(mine, pieces, last, *unread):
            kind = bf16 if pair_groups == 1 else f32
            body = rows_sum_body(mine, len(pieces))
            count = rows if mine else rows + extra
            (total,) = run("sum_gradient", body, [((count, part), kind)], [*pieces, last, *unread])
            if pair_groups > 1:
                sent = total.astype(bf16)
                others = [start(sent, along_g(dg)) for dg in range(1, pair_groups)]
                (total,) = run(
                    "add_groups", add_rows_body, [((count, part), bf16)], [total, *others]
                )
            return total

        def features_of(blocks, full, out):
            total = sum(
                jnp.dot(
                    block, full[dz * span : (dz + 1) * span, :], preferred_element_type=f32
                )
                for block, dz in zip(blocks, g_order)
            )
            out[...] = (total * feat ** (-0.5)).astype(bf16)

        def fill_body(*refs):
            z, y, core, q = place()
            for k in range(nz * ny):
                dz, dy = w_order[k // ny], k % ny
                ref, at = (refs[k], 0) if dz != 1 else (refs[-2], dy * 2 * rows)
                block = (z ^ turned(z, dz)) * ny + lax.rem(y + dy, ny)
                refs[-1][aligned(block, 2 * rows), :] = ref[at : at + 2 * rows, :]

        def near_body(own, sib, full, f_own, f_sib):
            for ref, out in ((own, f_own), (sib, f_sib)):
                features_of([ref[:, k * span : (k + 1) * span] for k in range(nz)], full, out)

        def far_body(*refs):
            features_of([ref[...] for ref in refs[:nz]], refs[nz], refs[nz + 1])

        def far_features(blocks):
            return run(
                "far_features", far_body, [((tokens, part), bf16)], [*blocks, w_full]
            )[0]

        def place_body(*refs):
            z, y, core, q = place()
            for j in range(4):
                refs[4][:, aligned(q ^ j, part)] = refs[j][...]

        w_order = [0, 3, 2, 1]
        others = range(1, ny)
        w_line = [None] * nz
        w_side = [None] * nz
        far_par, far_dia = [None] * nz, [None] * nz
        terms, moved_y = [None] * nz, [None] * nz

        def teacher_y(dz, *gates):
            w_side[dz] = [start(w_line[dz], along_y(-dy), *gates) for dy in others]

        def block_sum(dz, *parts, more=0):
            return add([terms[dz][0], *moved_y[dz], *parts], bf16, more)

        first, near_own, c_own, second, third, mark = run(
            "cut_tokens",
            cut_body,
            [
                ((count, width), bf16)
                for count, width in (
                    (tokens, lead + span), (tokens, feat + part), (tokens, part),
                    (tokens + 2 * extra, span), (tokens, 2 * span), (tokens, part),
                )
            ],
            [patches, cotangent],
        )
        w_same, w_other = run(
            "cast_teacher",
            cast_body,
            [((rows, part), bf16), ((4 * rows + 2 * extra, part), bf16)],
            [after(teacher, first)],
        )
        w_sib = start(w_other, sibling)
        message = start(first, partner)
        near_sib = start(near_own, sibling)
        (w_line[0],) = run(
            "join_teacher", join_body, [((2 * rows, part), bf16)], [w_same, w_sib]
        )
        w_line[3] = start(w_line[0], along_z(1))
        teacher_y(0)
        teacher_y(3, *w_side[0])
        (turn,) = run(
            "stack_teacher",
            stack_body,
            [((ny * 2 * rows + 2 * extra, part), bf16)],
            [after(w_line[0], near_sib), *w_side[0]],
        )
        w_line[2] = start(w_line[3], along_z(1))
        turn = start(turn, along_z(-1), w_line[2])
        block = start(second, partner)
        c_other, c_par, far_par[0] = run(
            "split_message",
            split_body,
            [((tokens, part), bf16)] * 2 + [((tokens, span), bf16)],
            [after(message, near_sib)],
        )
        c_dia = start(c_other, sibling)
        far_dia[0] = start(far_par[0], sibling)
        wait(*w_side[3])
        gradient_block(0)
        block_y(3)
        both = start(third, partner)
        (far_par[1],) = run("take_block", first_body, [((tokens, span), bf16)], [block])
        far_dia[1] = start(far_par[1], sibling)
        gradient_block(1)
        onward = block_sum(3, more=extra)
        block_y(2, onward)
        teacher_y(2, onward)
        onward = start(onward, across_z(1))
        *pieces, far_par[2], far_par[3] = run(
            "take_blocks",
            take_body,
            [((tokens // 2, span), bf16)] * 2 + [((tokens, span), bf16)] * 2,
            [after(both, turn)],
        )
        pieces = [start(piece, sibling) for piece in pieces]
        (far_dia[2],) = run("join_pieces", pieces_body, [((tokens, span), bf16)], pieces)
        gradient_block(2)
        block_y(1)
        onward = start(block_sum(2, onward), across_z(2))
        far_dia[3] = start(far_par[3], sibling, terms[1][0])
        (w_full,) = run(
            "fill_teacher",
            fill_body,
            [((feat, part), bf16)],
            [*(w for dz in w_order[:-1] for w in (w_line[dz], *w_side[dz])), turn],
        )
        f_par = start(far_features(far_par), partner)
        gradient_block(3)
        block_y(0)
        f_dia = start(far_features(far_dia), diagonal)
        back = run(
            "add_halves", halves_sum_body, [((rows, part), bf16)] * 2, [terms[1][0], *moved_y[1]]
        )
        back_other, back_mine = [start(half, across_z(1)) for half in back]
        f_own, f_sib = run(
            "near_features",
            near_body,
            [((tokens, part), bf16)] * 2,
            [near_own, near_sib, w_full],
        )
        f_sib = start(f_sib, sibling)
        wait(f_par, f_dia)
        pieces = [terms[0][0], *moved_y[0], onward]
        spacer = start(mark, sibling, onward)
        other = gradient_rows(False, pieces, back_other)
        g_dia, g_sib = start(other, diagonal), start(other, sibling)
        mine = gradient_rows(True, pieces, back_mine, spacer)
        g_par = start(mine, partner)
        def update_body(quarters):
            def body(*refs):
                z, y, core, q = place()
                student, first, second, teach = refs[len(quarters) :][:4]
                outs, held, sems = refs[-6:-2], refs[-2], refs[-1]
                corr_one = 1.0 - beta_one**STEP
                corr_two = 1.0 - beta_two**STEP
                copies = []
                for i, j in enumerate(quarters):
                    at = (slice(None), aligned(q ^ j, part))
                    gradient = refs[i][:rows, :].astype(f32)
                    new_first = beta_one * first[at] + (1.0 - beta_one) * gradient
                    new_second = beta_two * second[at] + (1.0 - beta_two) * gradient * gradient
                    direction = new_first / corr_one / (jnp.sqrt(new_second / corr_two) + adam_eps)
                    weights = student[at]
                    new_student = weights - learn_rate * (direction + decay_rate * weights)
                    new_teacher = ema_keep * teach[at] + (1.0 - ema_keep) * new_student
                    for k, new in enumerate((new_student, new_first, new_second, new_teacher)):
                        held[4 * i + k] = new
                        copies.append(
                            pltpu.make_async_copy(
                                held.at[4 * i + k], outs[k].at[at], sems.at[4 * i + k]
                            )
                        )
                        copies[-1].start()
                for copy in copies:
                    copy.wait()

            return body

        def update(name, quarters, grads, begun):
            inputs = [after(grads[0], *clock), *grads[1:]]
            inputs += [student, first_moment, second_moment, teacher]
            with jax.named_scope(name):
                out = pl.pallas_call(
                    update_body(quarters),
                    out_shape=[jax.ShapeDtypeStruct((rows, outw), f32)] * 4,
                    in_specs=[VMEM] * len(inputs) + [ANY] * len(begun),
                    out_specs=[ANY] * 4,
                    input_output_aliases={len(inputs) + k: k for k in range(len(begun))},
                    scratch_shapes=[
                        pltpu.VMEM((4 * len(quarters), rows, part), f32),
                        pltpu.SemaphoreType.DMA((4 * len(quarters),)),
                    ],
                    cost_estimate=pl.CostEstimate(flops=1, bytes_accessed=1, transcendentals=0),
                    compiler_params=pltpu.CompilerParams(vmem_limit_bytes=16 * 2**20),
                )(*inputs, *begun)
            clock[:] = out[:1]
            return out

        new = update("update_near", (0, 1), [mine, g_sib], [])
        (features,) = run(
            "place_features",
            place_body,
            [((tokens, outw), bf16)],
            [f_own, f_sib, f_par, f_dia],
        )
        new = update("update_partner", (2,), [g_par], new)
        new = update("update_diagonal", (3,), [g_dia], new)
        return (features, *new)

    tokens_placed, weights_placed = P(("fsdp", "rep"), None), P("fsdp", None)
    return jax.shard_map(
        per_device,
        mesh=mesh,
        in_specs=(tokens_placed,) * 2 + (weights_placed,) * 4,
        out_specs=(tokens_placed,) + (weights_placed,) * 4,
        check_vma=False,
    )
```

```python
import math

import jax
import jax.numpy as jnp
from jax import lax
from jax.experimental import pallas as pl
from jax.experimental.pallas import tpu as pltpu
from jax.sharding import PartitionSpec as P

STEP = 100

beta_one = 0.9
beta_two = 0.999
adam_eps = 1e-08
learn_rate = 0.1
decay_rate = 0.04
ema_keep = 0.994

bf16, f32 = jnp.bfloat16, jnp.float32
VMEM = pl.BlockSpec(memory_space=pltpu.VMEM)
ANY = pl.BlockSpec(memory_space=pl.ANY)


def call(name, body, outs, inputs, scratch=()):
    shapes = [jax.ShapeDtypeStruct(*out) for out in outs]
    moved = sum(a.size * a.dtype.itemsize for a in (*inputs, *shapes))
    held = sum(4 * math.prod(getattr(s, "shape", ())) for s in scratch)
    with jax.named_scope(name):
        return pl.pallas_call(
            body,
            out_shape=shapes,
            in_specs=[VMEM] * len(inputs),
            out_specs=[VMEM] * len(shapes),
            scratch_shapes=list(scratch),
            cost_estimate=pl.CostEstimate(flops=1, bytes_accessed=1, transcendentals=0),
            compiler_params=pltpu.CompilerParams(vmem_limit_bytes=moved + held + 4 * 2**20),
        )(*inputs)


def after(value, *others):
    return lax.optimization_barrier((value, *others))[0]


def aligned(index, size):
    return pl.ds(pl.multiple_of(index * size, size), size)


def solution(mesh):
    n, r = mesh.shape["fsdp"], mesh.shape["rep"]
    nz = 4
    ny = n // (2 * nz)
    pair_groups = r // 2

    def send(value, move):
        perm = []
        for f in range(n):
            for p in range(r):
                z, y, c = f // (2 * ny), f // 2 % ny, f % 2
                z, y, c, g, h = move(z, y, c, p // 2, p % 2)
                perm.append((f * r + p, ((z * ny + y) * 2 + c) * r + g * 2 + h))
        return lax.ppermute(value, ("fsdp", "rep"), perm)

    def sibling(z, y, c, g, h):
        return z, y, 1 - c, g, h

    def partner(z, y, c, g, h):
        return z, y, c, g, 1 - h

    def diagonal(z, y, c, g, h):
        return z, y, 1 - c, g, 1 - h

    def turned(z, d):
        p = ((z ^ (z >> 1)) + d) & 3
        return p ^ (p >> 1)

    def along_z(d):
        return lambda z, y, c, g, h: (turned(z, d), y, c, g, h)

    def across_z(d):
        return lambda z, y, c, g, h: (z ^ d, y, c, g, h)

    def along_y(d):
        return lambda z, y, c, g, h: (z, (y + d) % ny, c, g, h)

    def along_g(d):
        return lambda z, y, c, g, h: (z, y, c, (g + d) % pair_groups, h)

    def place():
        f = lax.axis_index("fsdp")
        core = lax.rem(f, 2)
        return f // (2 * ny), lax.rem(f // 2, ny), core, lax.rem(lax.axis_index("rep"), 2) * 2 + core

    def per_device(patches, cotangent, student, first_moment, second_moment, teacher):
        tokens, feat = patches.shape
        outw = cotangent.shape[1]
        rows = teacher.shape[0]
        part = outw // 4
        span = feat // nz
        g_order = [3, 2, 1, 0]
        lead = 2 * part
        extra = 16

        def cut_body(p, c, first, near, c_own, second, third, mark):
            z, y, core, q = place()
            mark[...] = c[: mark.shape[0], :part]
            first[:, :lead] = c[:, aligned(1 - q // 2, lead)]
            for k, dz in enumerate(g_order):
                block = p[:, aligned(z ^ dz, span)]
                near[:, k * span : (k + 1) * span] = block
                if k == 0:
                    first[:, lead:] = block
                elif k == 1:
                    second[:tokens, :] = block
                    second[tokens:, :] = block[: second.shape[0] - tokens, :]
                else:
                    third[:, (k - 2) * span : (k - 1) * span] = block
            near[:, feat:] = c[:, aligned(q ^ 1, part)]
            c_own[...] = c[:, aligned(q, part)]

        def split_body(message, c_sib, c_here, block):
            z, y, core, q = place()
            c_sib[...] = message[:, aligned(1 - core, part)]
            c_here[...] = message[:, aligned(core, part)]
            block[...] = message[:, lead:]

        def first_body(message, block):
            block[...] = message[:tokens, :]

        def take_body(message, upper, lower, first, second):
            first[...] = message[:, :span]
            second[...] = message[:, span:]
            upper[...] = message[: tokens // 2, :span]
            lower[...] = message[tokens // 2 :, :span]

        def pieces_body(upper, lower, block):
            block[: tokens // 2, :] = upper[...]
            block[tokens // 2 :, :] = lower[...]

        clock = []

        def run(name, body, outs, inputs, *scratch, **options):
            first = after(inputs[0], *clock) if clock else inputs[0]
            out = call(name, body, outs, [first, *inputs[1:]], *scratch, **options)
            clock[:] = out[:1]
            return out

        def start(value, move, *others):
            return send(after(value, *others) if others else value, move)

        def wait(*values):
            clock.extend(values)

        def cast_body(t, same, other):
            z, y, core, q = place()
            same[...] = t[:, aligned(q, part)].astype(bf16)
            other[:rows, :] = t[:, aligned(q ^ 1, part)].astype(bf16)
            other[rows:, :] = jnp.zeros((other.shape[0] - rows, part), bf16)

        def join_body(same, sib, out):
            z, y, core, q = place()
            out[aligned(core, rows), :] = same[...]
            out[aligned(1 - core, rows), :] = sib[:rows, :]

        def stack_body(*refs):
            for k, ref in enumerate(refs[:-1]):
                refs[-1][k * 2 * rows : (k + 1) * 2 * rows, :] = ref[...]
            refs[-1][ny * 2 * rows :, :] = refs[0][: 2 * extra, :]

        def terms_body(k):
            def body(own, sib, par, dia, c0, c_par, c_dia, *outs):
                z, y, core, q = place()
                whole = outs[-1]
                near = slice(k * span, (k + 1) * span)
                total = None
                for p, c in (
                    (own[:, near], c0[...]),
                    (sib[:, near], sib[:, feat:]),
                    (par[...], c_par[...]),
                    (dia[...], c_dia[...]),
                ):
                    term = lax.dot_general(
                        p, c, (((0,), (0,)), ((), ())), preferred_element_type=f32
                    )
                    total = term if total is None else total + term
                whole[...] = total
                for dy in range(ny):
                    block = whole[aligned(lax.rem(y + dy, ny), 2 * rows), :]
                    outs[dy][: 2 * rows, :] = block.astype(outs[dy].dtype)
                    if outs[dy].shape[0] > 2 * rows:
                        rest = (outs[dy].shape[0] - 2 * rows, part)
                        outs[dy][2 * rows :, :] = jnp.zeros(rest, outs[dy].dtype)

            return body

        def block_y(dz, *gates):
            moved_y[dz] = [start(terms[dz][dy], along_y(dy), *gates) for dy in others]

        def gradient_block(k):
            dz = g_order[k]
            terms[dz] = run(
                "gradient_block",
                terms_body(k),
                [((2 * rows, part), f32)]
                + [((2 * rows + extra * (k == 0), part), bf16)] * (ny - 1),
                [near_own, near_sib, far_par[k], far_dia[k], c_own, c_par, c_dia],
                scratch=[pltpu.VMEM((span, part), f32)],
            )

        def add_body(*refs):
            total = sum(ref[: 2 * rows, :].astype(f32) for ref in refs[:-1])
            refs[-1][: 2 * rows, :] = total.astype(refs[-1].dtype)
            if refs[-1].shape[0] > 2 * rows:
                rest = (refs[-1].shape[0] - 2 * rows, part)
                refs[-1][2 * rows :, :] = jnp.zeros(rest, refs[-1].dtype)

        def add(values, dtype, more=0):
            return run("add_blocks", add_body, [((2 * rows + more, part), dtype)], values)[0]

        def sum_body(*refs):
            z, y, core, q = place()
            for out, at in zip(refs[-2:], (aligned(core, rows), aligned(1 - core, rows))):
                out[...] = sum(ref[at, :].astype(f32) for ref in refs[:-3]).astype(bf16)

        def features_of(blocks, full, out):
            total = sum(
                jnp.dot(
                    block, full[dz * span : (dz + 1) * span, :], preferred_element_type=f32
                )
                for block, dz in zip(blocks, g_order)
            )
            out[...] = (total * feat ** (-0.5)).astype(bf16)

        def fill_body(*refs):
            z, y, core, q = place()
            for k in range(nz * ny):
                dz, dy = w_order[k // ny], k % ny
                ref, at = (refs[k], 0) if dz != 1 else (refs[-2], dy * 2 * rows)
                block = (z ^ turned(z, dz)) * ny + lax.rem(y + dy, ny)
                refs[-1][aligned(block, 2 * rows), :] = ref[at : at + 2 * rows, :]

        def near_body(own, sib, full, f_own, f_sib):
            for ref, out in ((own, f_own), (sib, f_sib)):
                features_of([ref[:, k * span : (k + 1) * span] for k in range(nz)], full, out)

        def far_body(*refs):
            features_of([ref[...] for ref in refs[:nz]], refs[nz], refs[nz + 1])

        def far_features(blocks):
            return run(
                "far_features", far_body, [((tokens, part), bf16)], [*blocks, w_full]
            )[0]

        def place_body(*refs):
            z, y, core, q = place()
            for j in range(4):
                refs[4][:, aligned(q ^ j, part)] = refs[j][...]

        w_order = [0, 3, 2, 1]
        others = range(1, ny)
        w_line = [None] * nz
        w_side = [None] * nz
        far_par, far_dia = [None] * nz, [None] * nz
        terms, moved_y = [None] * nz, [None] * nz

        def teacher_y(dz, *gates):
            w_side[dz] = [start(w_line[dz], along_y(-dy), *gates) for dy in others]

        def block_sum(dz, *parts, more=0):
            return add([terms[dz][0], *moved_y[dz], *parts], bf16, more)

        first, near_own, c_own, second, third, mark = run(
            "cut_tokens",
            cut_body,
            [
                ((count, width), bf16)
                for count, width in (
                    (tokens, lead + span), (tokens, feat + part), (tokens, part),
                    (tokens + 2 * extra, span), (tokens, 2 * span), (tokens - extra, part),
                )
            ],
            [patches, cotangent],
        )
        w_same, w_other = run(
            "cast_teacher",
            cast_body,
            [((rows, part), bf16), ((4 * rows + 2 * extra, part), bf16)],
            [after(teacher, first)],
        )
        w_sib = start(w_other, sibling)
        message = start(first, partner)
        near_sib = start(near_own, sibling)
        (w_line[0],) = run(
            "join_teacher", join_body, [((2 * rows, part), bf16)], [w_same, w_sib]
        )
        w_line[3] = start(w_line[0], along_z(1))
        teacher_y(0)
        teacher_y(3, *w_side[0])
        (turn,) = run(
            "stack_teacher",
            stack_body,
            [((ny * 2 * rows + 2 * extra, part), bf16)],
            [after(w_line[0], near_sib), *w_side[0]],
        )
        w_line[2] = start(w_line[3], along_z(1))
        turn = start(turn, along_z(-1), w_line[2])
        block = start(second, partner)
        c_other, c_par, far_par[0] = run(
            "split_message",
            split_body,
            [((tokens, part), bf16)] * 2 + [((tokens, span), bf16)],
            [after(message, near_sib)],
        )
        c_dia = start(c_other, sibling)
        far_dia[0] = start(far_par[0], sibling)
        wait(*w_side[3])
        gradient_block(0)
        block_y(3)
        both = start(third, partner)
        (far_par[1],) = run("take_block", first_body, [((tokens, span), bf16)], [block])
        far_dia[1] = start(far_par[1], sibling)
        gradient_block(1)
        onward = block_sum(3, more=extra)
        block_y(2, onward)
        teacher_y(2, onward)
        onward = start(onward, across_z(1))
        *pieces, far_par[2], far_par[3] = run(
            "take_blocks",
            take_body,
            [((tokens // 2, span), bf16)] * 2 + [((tokens, span), bf16)] * 2,
            [after(both, turn)],
        )
        pieces = [start(piece, sibling) for piece in pieces]
        (far_dia[2],) = run("join_pieces", pieces_body, [((tokens, span), bf16)], pieces)
        gradient_block(2)
        block_y(1)
        onward = start(block_sum(2, onward), across_z(2))
        far_dia[3] = start(far_par[3], sibling, terms[1][0])
        (w_full,) = run(
            "fill_teacher",
            fill_body,
            [((feat, part), bf16)],
            [*(w for dz in w_order[:-1] for w in (w_line[dz], *w_side[dz])), turn],
        )
        f_par = start(far_features(far_par), partner)
        gradient_block(3)
        block_y(0)
        f_dia = start(far_features(far_dia), diagonal)
        back = start(block_sum(1), across_z(1))
        f_own, f_sib = run(
            "near_features",
            near_body,
            [((tokens, part), bf16)] * 2,
            [near_own, near_sib, w_full],
        )
        f_sib = start(f_sib, sibling)
        wait(f_par, f_dia)
        pieces = [terms[0][0], *moved_y[0], onward, back]
        spacer = start(mark, sibling, onward)
        if pair_groups > 1:
            total = add(pieces, f32)
            sent = total.astype(bf16)
            pieces = [total] + [start(sent, along_g(dg)) for dg in range(1, pair_groups)]
        mine, other = run("sum_gradient", sum_body, [((rows, part), bf16)] * 2, [*pieces, spacer])
        g_par, g_dia, g_sib = (
            start(mine, partner), start(other, diagonal), start(other, sibling)
        )
        def update_body(quarters):
            def body(*refs):
                z, y, core, q = place()
                student, first, second, teach = refs[len(quarters) :][:4]
                outs, held, sems = refs[-6:-2], refs[-2], refs[-1]
                corr_one = 1.0 - beta_one**STEP
                corr_two = 1.0 - beta_two**STEP
                copies = []
                for i, j in enumerate(quarters):
                    at = (slice(None), aligned(q ^ j, part))
                    gradient = refs[i][...].astype(f32)
                    new_first = beta_one * first[at] + (1.0 - beta_one) * gradient
                    new_second = beta_two * second[at] + (1.0 - beta_two) * gradient * gradient
                    direction = new_first / corr_one / (jnp.sqrt(new_second / corr_two) + adam_eps)
                    weights = student[at]
                    new_student = weights - learn_rate * (direction + decay_rate * weights)
                    new_teacher = ema_keep * teach[at] + (1.0 - ema_keep) * new_student
                    for k, new in enumerate((new_student, new_first, new_second, new_teacher)):
                        held[4 * i + k] = new
                        copies.append(
                            pltpu.make_async_copy(
                                held.at[4 * i + k], outs[k].at[at], sems.at[4 * i + k]
                            )
                        )
                        copies[-1].start()
                for copy in copies:
                    copy.wait()

            return body

        def update(name, quarters, grads, begun):
            inputs = [after(grads[0], *clock), *grads[1:]]
            inputs += [student, first_moment, second_moment, teacher]
            with jax.named_scope(name):
                out = pl.pallas_call(
                    update_body(quarters),
                    out_shape=[jax.ShapeDtypeStruct((rows, outw), f32)] * 4,
                    in_specs=[VMEM] * len(inputs) + [ANY] * len(begun),
                    out_specs=[ANY] * 4,
                    input_output_aliases={len(inputs) + k: k for k in range(len(begun))},
                    scratch_shapes=[
                        pltpu.VMEM((4 * len(quarters), rows, part), f32),
                        pltpu.SemaphoreType.DMA((4 * len(quarters),)),
                    ],
                    cost_estimate=pl.CostEstimate(flops=1, bytes_accessed=1, transcendentals=0),
                    compiler_params=pltpu.CompilerParams(vmem_limit_bytes=16 * 2**20),
                )(*inputs, *begun)
            clock[:] = out[:1]
            return out

        new = update("update_near", (0, 1), [mine, g_sib], [])
        (features,) = run(
            "place_features",
            place_body,
            [((tokens, outw), bf16)],
            [f_own, f_sib, f_par, f_dia],
        )
        new = update("update_partner", (2,), [g_par], new)
        new = update("update_diagonal", (3,), [g_dia], new)
        return (features, *new)

    tokens_placed, weights_placed = P(("fsdp", "rep"), None), P("fsdp", None)
    return jax.shard_map(
        per_device,
        mesh=mesh,
        in_specs=(tokens_placed,) * 2 + (weights_placed,) * 4,
        out_specs=(tokens_placed,) + (weights_placed,) * 4,
        check_vma=False,
    )
```
